32 devices in a mesh: seq: 4 (over y, x), head: 4 (over z), rows: 2 (over core).
Axes of the slice: x: 2, y: 2, z: 4, core: 2. Of those that a mesh axis runs over, the one named last changes fastest.
Arguments:
- queries: bfloat16 [8, 4, 640, 2048], P('seq', None, 'rows', 'head'), may hold values from -6 to 6
- keys: bfloat16 [8, 4, 640, 2048], P('seq', None, 'rows', 'head'), may hold values from -6 to 6
- values: bfloat16 [8, 4, 640, 2048], P('seq', None, 'rows', 'head'), may hold values from -6 to 6
- counts: int32 [8], replicated, may hold values from 1 to 4, as said below
- rate: float32 [4], P('head'), may hold values from 0.125 to 1
- w_first: bfloat16 [4, 512, 256], P('head'), may hold values from -0.25 to 0.25
- w_third: bfloat16 [4, 512, 256], P('head'), may hold values from -0.25 to 0.25
- w_second: bfloat16 [4, 256, 512], P('head'), may hold values from -0.375 to 0.375
Outputs:
- mixed: bfloat16 [8, 4, 640, 2048], P('seq', None, 'rows', 'head')
The draws below stay inside these ranges and needn't reach their ends.
Inputs may be any that keep to these rules, and one draw needn't show every extreme that they name: `counts`: taken in order, the sequences fall into consecutive runs, as many as there are groups of 2 sequences, each run with exactly 4 blocks in all; some sequence has 4 blocks.
All inputs are finite; a program needn't handle non-finite values.
Results may differ from the reference program's by a relative error of at most 0.02.
Values may be sent and summed in bfloat16 or wider, within the bound.
A program may use at most 64 MiB of HBM per device.

```python
import math
import jax
import jax.numpy as jnp
from jax import lax

D = 2048
HEADS = 4
HD = 512
FH = 256
BLOCK_DEV = 320
BLOCKS = 4
SLOTS = 2
SEQS = 8
BLOCK = 640
N_ROWS = 2


def draw_counts(key, part):
    key = jax.random.fold_in(jax.random.fold_in(key, 7919), part)
    groups = SEQS // SLOTS
    lone_group = jax.random.randint(jax.random.fold_in(key, 11), (), 0, groups)
    group_sizes = jnp.ones((groups,), jnp.int32)
    group_ids = jnp.arange(groups, dtype=jnp.int32)
    for attempt in range(SEQS - groups):
        scores = jax.random.permutation(jax.random.fold_in(key, 100 + attempt), groups).astype(jnp.int32)
        has_room = (group_sizes < BLOCKS) & (group_ids != lone_group)
        chosen = jnp.argmax(jnp.where(has_room, scores, -1))
        group_sizes = group_sizes.at[chosen].add(1)
    run_ends = jnp.cumsum(group_sizes)
    position = jnp.arange(SEQS, dtype=jnp.int32)
    member_of = jnp.sum((position[:, None] >= run_ends[None, :]).astype(jnp.int32), axis=1)
    member = member_of[:, None] == group_ids[None, :]
    counts = jnp.ones((SEQS,), jnp.int32)
    for attempt in range(BLOCKS - 1):
        totals = jnp.sum(jnp.where(member, counts[:, None], 0), axis=0)
        scores = jax.random.permutation(jax.random.fold_in(key, 500 + attempt), SEQS).astype(jnp.int32)
        chosen = jnp.argmax(jnp.where(member, scores[:, None], -1), axis=0)
        counts = counts.at[chosen].add((totals < BLOCKS).astype(jnp.int32))
    return counts.astype(jnp.int32)


def level_of(own_key, extent, pieces, low, largest):
    def one(axis_at, parts):
        heights = jax.random.uniform(jax.random.fold_in(jax.random.fold_in(own_key, 6), axis_at), (parts,), jnp.float32, low / len(pieces), largest / len(pieces))
        return jnp.repeat(jnp.exp(heights), extent[axis_at] // parts).reshape((-1,) + (1,) * (len(extent) - axis_at - 1))

    factor_of = one(*pieces[0])
    for cut in pieces[1:]:
        factor_of = factor_of * one(*cut)
    return factor_of


def scatter_about(own_key, dims, deviation, limit, pieces=(), kind=jnp.bfloat16):
    array = jax.random.normal(own_key, dims, jnp.float32) * deviation
    if len(pieces) > 0:
        array = level_of(own_key, dims, pieces, -0.22, 0.18) * array
    return jnp.clip(array, min=-limit, max=limit).astype(kind)


def setup_inputs(seed: int = 0) -> dict:
    key_of = jax.random.split(jax.random.key(seed), 9)
    return {
        "queries": scatter_about(key_of[0], (SEQS, BLOCKS, BLOCK, D), 1.0, 6.0, ((0, 4), (2, 2), (3, 4))),
        "keys": scatter_about(key_of[1], (SEQS, BLOCKS, BLOCK, D), 1.0, 6.0, ((0, 4), (2, 2), (3, 4))),
        "values": scatter_about(key_of[2], (SEQS, BLOCKS, BLOCK, D), 1.0, 6.0, ((0, 4), (2, 2), (3, 4))),
        "counts": draw_counts(jax.random.fold_in(key_of[8], 71), 0),
        "rate": jnp.clip(jnp.exp(math.log(1.0) - 2.0794415 * jax.random.uniform(key_of[4], (HEADS,), jnp.float32) ** level_of(key_of[4], (HEADS,), ((0, 4),), -0.2, 0.2)), 0.125, 1.0),
        "w_first": scatter_about(key_of[5], (HEADS, HD, FH), HD ** -0.5, 0.25, ((0, 4),)),
        "w_third": scatter_about(key_of[6], (HEADS, HD, FH), HD ** -0.5, 0.25, ((0, 4),)),
        "w_second": scatter_about(key_of[7], (HEADS, FH, HD), FH ** -0.5, 0.375, ((0, 4),)),
    }


def normalize_rows(matrix, epsilon):
    matrix = matrix.astype(jnp.float32)
    return matrix * lax.rsqrt(lax.optimization_barrier(jnp.mean(matrix * matrix, axis=-1, keepdims=True)) + epsilon)

def column_norms(weight, axis_in):
    return jnp.sqrt(lax.optimization_barrier(jnp.sum(weight * weight, axis=axis_in)) + 1e-06)

def rescale(moved, target, axis_in):
    return moved * (jnp.expand_dims(target, axis_in) / jnp.expand_dims(column_norms(moved, axis_in), axis_in))

def rounded(matrix):
    return lax.optimization_barrier(matrix.astype(jnp.bfloat16)).astype(jnp.float32)

def block_sums(first_op, second_op):
    heads = first_op.shape[0]
    first_runs = first_op.reshape(heads, N_ROWS, BLOCK_DEV, first_op.shape[-1]).astype(jnp.float32)
    second_runs = second_op.reshape(heads, N_ROWS, BLOCK_DEV, second_op.shape[-1]).astype(jnp.float32)
    partial_sums = jnp.einsum('hnra,hnrb->hnab', first_runs, second_runs)
    return lax.optimization_barrier(jnp.sum(rounded(partial_sums), axis=1))

def reference(queries, keys, values, counts, rate, w_first, w_third, w_second):
    heads, head_width, hidden_units = w_first.shape
    start_weights = (w_first.astype(jnp.float32), w_third.astype(jnp.float32), w_second.astype(jnp.float32))
    targets = tuple((column_norms(weight, 1) for weight in start_weights))
    step_rate = (rate / BLOCK)[:, None, None]

    def split_heads(block_rows):
        return block_rows.reshape(BLOCK, heads, head_width).transpose(1, 0, 2)

    def one_sequence(inputs):
        seq_queries, seq_keys, seq_values, length = inputs

        def advance(master, step_inputs):
            query_rows, key_rows, value_rows, block_index = step_inputs
            is_live = block_index < length
            current = tuple((rounded(weight) for weight in master))
            key_norm = normalize_rows(split_heads(key_rows), 1e-06).astype(jnp.bfloat16)
            key_float = key_norm.astype(jnp.float32)
            gate_pre = jnp.einsum('hrd,hdf->hrf', key_float, current[0])
            up_pre = jnp.einsum('hrd,hdf->hrf', key_float, current[1])
            gate_sig = jax.nn.sigmoid(gate_pre)
            gate_act = gate_pre * gate_sig
            hidden = (gate_act * up_pre).astype(jnp.bfloat16)
            value_heads = split_heads(value_rows)
            d_hidden = jnp.einsum('hrd,hfd->hrf', value_heads.astype(jnp.float32), current[2])
            d_gate = (d_hidden * up_pre * gate_sig * (1.0 + gate_pre * (1.0 - gate_sig))).astype(jnp.bfloat16)
            d_up = (d_hidden * gate_act).astype(jnp.bfloat16)
            sums = (block_sums(key_norm, d_gate), block_sums(key_norm, d_up), block_sums(hidden, value_heads))
            moved = tuple((rescale(weight + step_rate * grad_total, target, 1) for weight, grad_total, target in zip(master, sums, targets)))
            master = tuple((jnp.where(is_live, new_w, old_w) for new_w, old_w in zip(moved, master)))
            current = tuple((rounded(weight) for weight in master))
            query_float = rounded(normalize_rows(split_heads(query_rows), 1e-06))
            out_gate = jnp.einsum('hrd,hdf->hrf', query_float, current[0])
            out_up = jnp.einsum('hrd,hdf->hrf', query_float, current[1])
            out_hidden = rounded(out_gate * jax.nn.sigmoid(out_gate) * out_up)
            output = jnp.einsum('hrf,hfd->hrd', out_hidden, current[2])
            output = normalize_rows(output, 1e-05).astype(jnp.bfloat16)
            merged = output.transpose(1, 0, 2).reshape(BLOCK, heads * head_width)
            return (master, jnp.where(is_live, merged, jnp.zeros_like(merged)))
        block_ids = jnp.arange(BLOCKS, dtype=jnp.int32)
        _, outputs = lax.scan(advance, start_weights, (seq_queries, seq_keys, seq_values, block_ids))
        return outputs
    return lax.map(one_sequence, (queries, keys, values, counts))
```

```python
import functools

import jax
import jax.numpy as jnp
from jax import lax
from jax.experimental import pallas as pl
from jax.experimental.pallas import tpu as pltpu
from jax.sharding import PartitionSpec as P

MESH = pl.DeviceIdType.MESH
VMEM_LIMIT = 60 * 1024 * 1024


def matmul(first_op, second_op):
    return jnp.dot(first_op, second_op, preferred_element_type=jnp.float32)


def matmul_nt(first_op, second_op):
    return lax.dot_general(
        first_op, second_op, (((1,), (1,)), ((), ())), preferred_element_type=jnp.float32
    )


def unit_rows(matrix, epsilon):
    matrix = matrix.astype(jnp.float32)
    mean = jnp.mean(matrix * matrix, axis=-1, keepdims=True)
    return (matrix * lax.rsqrt(mean + epsilon)).astype(jnp.bfloat16)


def sigmoid(x):
    return 0.5 * jnp.tanh(0.5 * x) + 0.5


def chain_kernel(
    steps, slots, blocks, row_devices,
    counts_ref, rate_ref, q_hbm, k_hbm, v_hbm, w1_ref, w3_ref, w2_ref, out_ref,
    q_in, k_in, v_in, k_all, v_all, n_own, n_peer, state, sums_own, sums_peer,
    norm13, norm2, load_sem, send_sem, recv_sem,
):
    rows = q_in.shape[1]
    half = w2_ref.shape[1] // 2
    me = lax.axis_index("rows")
    peer = {"rows": 1 - me}
    seq = lax.axis_index("seq")
    step_rate = rate_ref[0] / (rows * row_devices)
    total_blocks = slots * blocks

    def local(src, dst, at):
        return pltpu.make_async_copy(src, dst, load_sem.at[at])

    first = pl.ds(0, 1)
    rest = pl.ds(1, total_blocks - 1)
    loads = [
        local(k_hbm.at[first], k_in.at[first], 0),
        local(v_hbm.at[first], v_in.at[first], 1),
        local(k_hbm.at[rest], k_in.at[rest], 2),
        local(v_hbm.at[rest], v_in.at[rest], 3),
        local(q_hbm, q_in, 4),
    ]
    for load in loads:
        load.start()

    barrier = pltpu.get_barrier_semaphore()
    pl.semaphore_signal(barrier, inc=1, device_id=peer, device_id_type=MESH)

    def where_at(t):
        block = jnp.int32(0)
        begins = t == 0
        offset = jnp.int32(0)
        for slot in range(slots):
            begins = begins | (t == offset)
            inside = jnp.minimum(jnp.maximum(t - offset, 0), blocks - 1)
            block = jnp.where(t >= offset, slot * blocks + inside, block)
            offset = offset + counts_ref[seq * slots + slot]
        return block, begins

    def remote(src, dst, kind, t):
        return pltpu.make_async_remote_copy(
            src_ref=src, dst_ref=dst, send_sem=send_sem.at[kind, t], recv_sem=recv_sem.at[kind, t],
            device_id=peer, device_id_type=MESH,
        )

    mine, theirs = pl.ds(0, rows), pl.ds(rows, rows)
    gates, downs = pl.ds(0, 2 * half), pl.ds(2 * half, half)

    def key_copy(t):
        return remote(k_all.at[t, mine], k_all.at[t, theirs], 0, t)

    def value_copy(t):
        return remote(v_all.at[t, mine], v_all.at[t, theirs], 1, t)

    def sums_copy(t):
        return remote(sums_own.at[t], sums_peer.at[t], 2, t)

    def gates_copy(t):
        return remote(n_own.at[t + 1, gates], n_peer.at[t, gates], 3, t)

    def downs_copy(t):
        return remote(n_own.at[t + 1, downs], n_peer.at[t, downs], 4, t)

    def prepare(t, block):
        v_all[t, mine] = v_in[block]
        value_copy(t).start()
        k_all[t, mine] = unit_rows(k_in[block], 1e-06)
        key_copy(t).start()

    units = pl.ds(pl.multiple_of(me * half, half), half)
    start_1 = w1_ref[0, :, units].astype(jnp.float32).T
    start_3 = w3_ref[0, :, units].astype(jnp.float32).T
    start_2 = w2_ref[0, units, :].astype(jnp.float32)
    start = jnp.concatenate([start_1, start_3, start_2], axis=0)
    state[0] = start
    n_own[0] = start.astype(jnp.bfloat16)
    start_13 = start[: 2 * half]
    norm13[...] = jnp.sqrt(jnp.sum(start_13 * start_13, axis=1, keepdims=True) + 1e-06)
    full_2 = w2_ref[0].astype(jnp.float32)
    norm2[...] = jnp.sqrt(jnp.sum(full_2 * full_2, axis=0, keepdims=True) + 1e-06)

    loads[0].wait()
    loads[1].wait()
    pl.semaphore_wait(barrier, 1)
    prepare(0, 0)
    for load in loads[2:]:
        load.wait()

    def answer(t):
        block, _ = where_at(t)
        query = unit_rows(q_in[block], 1e-06)
        own, other = n_own[t + 1], n_peer[t]
        hidden = []
        for weights in (own, other):
            both = matmul_nt(query, weights[: 2 * half])
            gate, up = both[:, :half], both[:, half:]
            hidden.append((gate * sigmoid(gate) * up).astype(jnp.bfloat16))
        result = matmul(
            jnp.concatenate(hidden, axis=1),
            jnp.concatenate([own[2 * half :], other[2 * half :]], axis=0),
        )
        out_ref[t] = unit_rows(result, 1e-05)

    def step(t, carry):
        @pl.when(t + 1 < steps)
        def _():
            prepare(t + 1, where_at(t + 1)[0])

        _, begins = where_at(t)
        from_state = jnp.where(begins, 0, 1)
        from_n = jnp.where(begins, 0, t)
        key_copy(t).wait_recv()
        value_copy(t).wait_recv()
        keys, values = k_all[t], v_all[t]
        both = matmul_nt(n_own[from_n, gates], keys)
        d_hidden = matmul_nt(n_own[from_n, downs], values)
        gate, up = both[:half], both[half:]
        sig = sigmoid(gate)
        act = gate * sig
        hidden = (act * up).astype(jnp.bfloat16)
        d_gate = (d_hidden * up * (sig + act - act * sig)).astype(jnp.bfloat16)
        d_up = (d_hidden * act).astype(jnp.bfloat16)

        moved_2 = state[from_state, downs] + step_rate * matmul(hidden, values)
        squares = moved_2 * moved_2
        sums_own[t] = jnp.sum(squares.reshape(half // 8, 8, squares.shape[1]), axis=0)
        sums_copy(t).start()

        moved_13 = state[from_state, gates] + step_rate * matmul(
            jnp.concatenate([d_gate, d_up], axis=0), keys
        )
        norm = jnp.sum(moved_13 * moved_13, axis=1, keepdims=True) + 1e-06
        new_13 = moved_13 * (norm13[...] * lax.rsqrt(norm))
        state[1, gates] = new_13
        state[1, downs] = moved_2
        n_own[t + 1, gates] = new_13.astype(jnp.bfloat16)
        gates_copy(t).start()

        @pl.when(t > 0)
        def _():
            gates_copy(t - 1).wait_recv()
            downs_copy(t - 1).wait_recv()
            answer(t - 1)

        sums_copy(t).wait_recv()
        norm = jnp.sum(sums_own[t] + sums_peer[t], axis=0, keepdims=True) + 1e-06
        new_2 = state[1, downs] * (norm2[...] * lax.rsqrt(norm))
        state[1, downs] = new_2
        n_own[t + 1, downs] = new_2.astype(jnp.bfloat16)
        downs_copy(t).start()
        return carry

    lax.fori_loop(0, steps, step, 0)
    last = steps - 1
    gates_copy(last).wait_recv()
    downs_copy(last).wait_recv()
    answer(last)

    def finish(t, carry):
        for copy in (key_copy, value_copy, sums_copy, gates_copy, downs_copy):
            copy(t).wait_send()
        return carry

    lax.fori_loop(0, steps, finish, 0)


def chain(steps, collective_id, queries, keys, values, counts, rate, w_first, w_third, w_second):
    slots, blocks, rows, width = queries.shape
    row_devices = lax.axis_size("rows")
    hidden = w_second.shape[1]
    half = hidden // 2
    total = slots * blocks
    flat = (total, rows, width)
    smem = pl.BlockSpec(memory_space=pltpu.SMEM)
    vmem = pl.BlockSpec(memory_space=pltpu.VMEM)
    hbm = pl.BlockSpec(memory_space=pl.ANY)
    bf16, f32 = jnp.bfloat16, jnp.float32
    return pl.pallas_call(
        functools.partial(chain_kernel, steps, slots, blocks, row_devices),
        out_shape=jax.ShapeDtypeStruct(flat, bf16),
        in_specs=[smem, smem, hbm, hbm, hbm, vmem, vmem, vmem],
        out_specs=vmem,
        scratch_shapes=[
            pltpu.VMEM(flat, bf16),
            pltpu.VMEM(flat, bf16),
            pltpu.VMEM(flat, bf16),
            pltpu.VMEM((steps, 2 * rows, width), bf16),
            pltpu.VMEM((steps, 2 * rows, width), bf16),
            pltpu.VMEM((steps + 1, 3 * half, width), bf16),
            pltpu.VMEM((steps, 3 * half, width), bf16),
            pltpu.VMEM((2, 3 * half, width), f32),
            pltpu.VMEM((steps, 8, width), f32),
            pltpu.VMEM((steps, 8, width), f32),
            pltpu.VMEM((2 * half, 1), f32),
            pltpu.VMEM((1, width), f32),
            pltpu.SemaphoreType.DMA((5,)),
            pltpu.SemaphoreType.DMA((5, steps)),
            pltpu.SemaphoreType.DMA((5, steps)),
        ],
        compiler_params=pltpu.CompilerParams(
            collective_id=collective_id, has_side_effects=True, vmem_limit_bytes=VMEM_LIMIT
        ),
        cost_estimate=pl.CostEstimate(
            flops=steps * 18 * rows * width * hidden,
            bytes_accessed=4 * 2 * total * rows * width,
            transcendentals=steps * 2 * rows * hidden,
        ),
        name="chain",
    )(
        counts, rate, queries.reshape(flat), keys.reshape(flat), values.reshape(flat),
        w_first, w_third, w_second,
    )


def pair_body(queries, keys, values, counts, rate, w_first, w_third, w_second):
    slots, blocks, rows, width = queries.shape
    total = slots * blocks
    in_order = chain(total, 0, queries, keys, values, counts, rate, w_first, w_third, w_second)
    group = lax.axis_index("seq")
    own_counts = lax.dynamic_slice_in_dim(counts, group * slots, slots)
    block_ids = jnp.arange(blocks, dtype=jnp.int32)
    parts = []
    offset = jnp.int32(0)
    for slot in range(slots):
        part = lax.dynamic_slice_in_dim(in_order, offset, blocks)
        live = (block_ids < own_counts[slot])[:, None, None]
        parts.append(jnp.where(live, part, jnp.zeros_like(part)))
        offset = offset + own_counts[slot]
    return jnp.stack(parts)


def normalize_rows(matrix, epsilon):
    matrix = matrix.astype(jnp.float32)
    return matrix * lax.rsqrt(jnp.mean(matrix * matrix, axis=-1, keepdims=True) + epsilon)


def column_norms(weight):
    return jnp.sqrt(jnp.sum(weight * weight, axis=0) + 1e-06)


def rescale(moved, target):
    return moved * (target[None, :] / column_norms(moved)[None, :])


def product(first_op, second_op):
    return jnp.dot(first_op, second_op, preferred_element_type=jnp.float32)


def contract_rows(first_op, second_op):
    return lax.dot_general(
        first_op, second_op, (((0,), (0,)), ((), ())), preferred_element_type=jnp.float32
    )


def against_rows(first_op, second_op):
    return lax.dot_general(
        first_op, second_op, (((1,), (1,)), ((), ())), preferred_element_type=jnp.float32
    )


def partial_sums(current, key_rows, value_rows):
    key_norm = normalize_rows(key_rows, 1e-06).astype(jnp.bfloat16)
    gate_pre = product(key_norm, current[0])
    up_pre = product(key_norm, current[1])
    gate_sig = jax.nn.sigmoid(gate_pre)
    gate_act = gate_pre * gate_sig
    hidden = (gate_act * up_pre).astype(jnp.bfloat16)
    d_hidden = against_rows(value_rows, current[2])
    d_gate = (d_hidden * up_pre * gate_sig * (1.0 + gate_pre * (1.0 - gate_sig))).astype(
        jnp.bfloat16
    )
    d_up = (d_hidden * gate_act).astype(jnp.bfloat16)
    return (
        contract_rows(key_norm, d_gate),
        contract_rows(key_norm, d_up),
        contract_rows(hidden, value_rows),
    )


def answer(current, query_rows):
    query_norm = normalize_rows(query_rows, 1e-06).astype(jnp.bfloat16)
    out_gate = product(query_norm, current[0])
    out_up = product(query_norm, current[1])
    out_hidden = (out_gate * jax.nn.sigmoid(out_gate) * out_up).astype(jnp.bfloat16)
    return normalize_rows(product(out_hidden, current[2]), 1e-05).astype(jnp.bfloat16)


def body(queries, keys, values, counts, rate, w_first, w_third, w_second):
    seq_slots, blocks, block_rows, head_width = queries.shape
    group_index = lax.axis_index("seq")
    row_devices = lax.axis_size("rows")
    step_rate = rate[0] / (block_rows * row_devices)
    initial = (w_first[0], w_third[0], w_second[0])
    full_master = tuple((weight.astype(jnp.float32) for weight in initial))
    full_targets = tuple((column_norms(weight) for weight in full_master))

    def combine(partials):
        return (
            lax.psum(partials[0].astype(jnp.bfloat16), "rows").astype(jnp.float32),
            lax.psum(partials[1].astype(jnp.bfloat16), "rows").astype(jnp.float32),
            lax.psum(partials[2].astype(jnp.bfloat16), "rows").astype(jnp.float32),
        )

    def refresh(master):
        as_bf16 = tuple((weight.astype(jnp.bfloat16) for weight in master))
        return as_bf16

    def advance(state_pair, step_inputs):
        master, current = state_pair
        query_rows, key_rows, value_rows, restart, is_live = step_inputs
        master = tuple(
            (
                jnp.where(restart, fresh_value, kept_value)
                for fresh_value, kept_value in zip(full_master, master)
            )
        )
        current = tuple(
            (
                jnp.where(restart, fresh_value, kept_value)
                for fresh_value, kept_value in zip(initial, current)
            )
        )
        totals = combine(partial_sums(current, key_rows, value_rows))
        moved = tuple(
            (
                rescale(weight + step_rate * grad_total, target)
                for weight, grad_total, target in zip(master, totals, full_targets)
            )
        )
        master = tuple((jnp.where(is_live, new_w, old_w) for new_w, old_w in zip(moved, master)))
        current = refresh(master)
        output = answer(current, query_rows)
        return ((master, current), jnp.where(is_live, output, jnp.zeros_like(output)))

    start_pair = (full_master, initial)
    flat_shape = (seq_slots * blocks, block_rows, head_width)
    block_ids = jnp.arange(blocks, dtype=jnp.int32)
    local_counts = lax.dynamic_slice_in_dim(counts, group_index * seq_slots, seq_slots)
    restart = jnp.tile(block_ids == 0, seq_slots)
    is_live = (block_ids[None, :] < local_counts[:, None]).reshape(-1)
    inputs = (
        queries.reshape(flat_shape),
        keys.reshape(flat_shape),
        values.reshape(flat_shape),
        restart,
        is_live,
    )
    _, outputs = lax.scan(advance, start_pair, inputs)
    return outputs.reshape(queries.shape)


def any_body(queries, keys, values, counts, rate, w_first, w_third, w_second):
    pair = lax.axis_size("rows") == 2 and w_second.shape[1] % 256 == 0 and queries.shape[2] % 16 == 0
    form = pair_body if pair else body
    return form(queries, keys, values, counts, rate, w_first, w_third, w_second)


def solution(mesh):
    return jax.shard_map(
        any_body,
        mesh=mesh,
        in_specs=(
            P("seq", None, "rows", "head"),
            P("seq", None, "rows", "head"),
            P("seq", None, "rows", "head"),
            P(),
            P("head"),
            P("head", None, None),
            P("head", None, None),
            P("head", None, None),
        ),
        out_specs=P("seq", None, "rows", "head"),
        check_vma=False,
    )
```

```python
import functools

import jax
import jax.numpy as jnp
from jax import lax
from jax.experimental import pallas as pl
from jax.experimental.pallas import tpu as pltpu
from jax.sharding import PartitionSpec as P

MESH = pl.DeviceIdType.MESH
VMEM_LIMIT = 60 * 1024 * 1024


def matmul(first_op, second_op):
    return jnp.dot(first_op, second_op, preferred_element_type=jnp.float32)


def matmul_nt(first_op, second_op):
    return lax.dot_general(
        first_op, second_op, (((1,), (1,)), ((), ())), preferred_element_type=jnp.float32
    )


def unit_rows(matrix, epsilon):
    matrix = matrix.astype(jnp.float32)
    mean = jnp.mean(matrix * matrix, axis=-1, keepdims=True)
    return (matrix * lax.rsqrt(mean + epsilon)).astype(jnp.bfloat16)


def sigmoid(x):
    return 0.5 * jnp.tanh(0.5 * x) + 0.5


def chain_kernel(
    steps, slots, blocks, row_devices,
    counts_ref, rate_ref, q_hbm, k_hbm, v_hbm, w1_ref, w3_ref, w2_ref, out_ref,
    q_in, k_in, v_in, k_all, v_all, n_own, n_peer, state, sums_own, sums_peer,
    norm13, norm2, out_all, load_sem, send_sem, recv_sem, out_sem,
):
    rows = q_in.shape[1]
    half = w2_ref.shape[1] // 2
    me = lax.axis_index("rows")
    peer = {"rows": 1 - me}
    seq = lax.axis_index("seq")
    step_rate = rate_ref[0] / (rows * row_devices)
    total_blocks = slots * blocks

    def local(src, dst, at):
        return pltpu.make_async_copy(src, dst, load_sem.at[at])

    first = pl.ds(0, 1)
    rest = pl.ds(1, total_blocks - 1)
    loads = [
        local(k_hbm.at[first], k_in.at[first], 0),
        local(v_hbm.at[first], v_in.at[first], 1),
        local(k_hbm.at[rest], k_in.at[rest], 2),
        local(v_hbm.at[rest], v_in.at[rest], 3),
        local(q_hbm, q_in, 4),
    ]
    for load in loads:
        load.start()

    barrier = pltpu.get_barrier_semaphore()
    pl.semaphore_signal(barrier, inc=1, device_id=peer, device_id_type=MESH)

    def where_at(t):
        block = jnp.int32(0)
        begins = t == 0
        offset = jnp.int32(0)
        for slot in range(slots):
            begins = begins | (t == offset)
            inside = jnp.minimum(jnp.maximum(t - offset, 0), blocks - 1)
            block = jnp.where(t >= offset, slot * blocks + inside, block)
            offset = offset + counts_ref[seq * slots + slot]
        return block, begins

    def remote(src, dst, kind, t):
        return pltpu.make_async_remote_copy(
            src_ref=src, dst_ref=dst, send_sem=send_sem.at[kind, t], recv_sem=recv_sem.at[kind, t],
            device_id=peer, device_id_type=MESH,
        )

    mine, theirs = pl.ds(0, rows), pl.ds(rows, rows)
    gates, downs = pl.ds(0, 2 * half), pl.ds(2 * half, half)

    def key_copy(t):
        return remote(k_all.at[t, mine], k_all.at[t, theirs], 0, t)

    def value_copy(t):
        return remote(v_all.at[t, mine], v_all.at[t, theirs], 1, t)

    def sums_copy(t):
        return remote(sums_own.at[t], sums_peer.at[t], 2, t)

    def gates_copy(t):
        return remote(n_own.at[t + 1, gates], n_peer.at[t, gates], 3, t)

    def downs_copy(t):
        return remote(n_own.at[t + 1, downs], n_peer.at[t, downs], 4, t)

    def prepare(t, block):
        v_all[t, mine] = v_in[block]
        k_all[t, mine] = unit_rows(k_in[block], 1e-06)

    def hand_over(t):
        key_copy(t).start()
        value_copy(t).start()

    def out_copy(t):
        return pltpu.make_async_copy(out_all.at[t], out_ref.at[t], out_sem.at[t])

    units = pl.ds(pl.multiple_of(me * half, half), half)
    start_1 = w1_ref[0, :, units].astype(jnp.float32).T
    start_3 = w3_ref[0, :, units].astype(jnp.float32).T
    start_2 = w2_ref[0, units, :].astype(jnp.float32)
    start = jnp.concatenate([start_1, start_3, start_2], axis=0)
    state[0] = start
    n_own[0] = start.astype(jnp.bfloat16)
    start_13 = start[: 2 * half]
    norm13[...] = jnp.sqrt(jnp.sum(start_13 * start_13, axis=1, keepdims=True) + 1e-06)
    full_2 = w2_ref[0].astype(jnp.float32)
    norm2[...] = jnp.sqrt(jnp.sum(full_2 * full_2, axis=0, keepdims=True) + 1e-06)

    loads[0].wait()
    loads[1].wait()
    pl.semaphore_wait(barrier, 1)
    prepare(0, 0)
    hand_over(0)
    for load in loads[2:]:
        load.wait()

    def answer(t):
        block, _ = where_at(t)
        query = unit_rows(q_in[block], 1e-06)
        own, other = n_own[t + 1], n_peer[t]
        hidden = []
        for weights in (own, other):
            both = matmul_nt(query, weights[: 2 * half])
            gate, up = both[:, :half], both[:, half:]
            hidden.append((gate * sigmoid(gate) * up).astype(jnp.bfloat16))
        result = matmul(
            jnp.concatenate(hidden, axis=1),
            jnp.concatenate([own[2 * half :], other[2 * half :]], axis=0),
        )
        out_all[t] = unit_rows(result, 1e-05)

    def step(t, has_before, has_after):
        _, begins = where_at(t)
        from_state = jnp.where(begins, 0, 1)
        from_n = jnp.where(begins, 0, t)
        key_copy(t).wait_recv()
        value_copy(t).wait_recv()
        keys, values = k_all[t], v_all[t]
        both = matmul_nt(n_own[from_n, gates], keys)
        d_hidden = matmul_nt(n_own[from_n, downs], values)
        if has_after:
            prepare(t + 1, where_at(t + 1)[0])
        gate, up = both[:half], both[half:]
        sig = sigmoid(gate)
        act = gate * sig
        hidden = (act * up).astype(jnp.bfloat16)
        d_gate = (d_hidden * up * (sig + act - act * sig)).astype(jnp.bfloat16)
        d_up = (d_hidden * act).astype(jnp.bfloat16)

        moved_2 = state[from_state, downs] + step_rate * matmul(hidden, values)
        squares = moved_2 * moved_2
        sums_own[t] = jnp.sum(squares.reshape(half // 8, 8, squares.shape[1]), axis=0)
        sums_copy(t).start()
        if has_after:
            hand_over(t + 1)
        if has_before:
            gates_copy(t - 1).wait_recv()
            downs_copy(t - 1).wait_recv()

        moved_13 = state[from_state, gates] + step_rate * matmul(
            jnp.concatenate([d_gate, d_up], axis=0), keys
        )
        norm = jnp.sum(moved_13 * moved_13, axis=1, keepdims=True) + 1e-06
        new_13 = moved_13 * (norm13[...] * lax.rsqrt(norm))
        state[1, gates] = new_13
        state[1, downs] = moved_2
        n_own[t + 1, gates] = new_13.astype(jnp.bfloat16)
        if has_before:
            answer(t - 1)
            out_copy(t - 1).start()
        gates_copy(t).start()

        sums_copy(t).wait_recv()
        norm = jnp.sum(sums_own[t] + sums_peer[t], axis=0, keepdims=True) + 1e-06
        new_2 = state[1, downs] * (norm2[...] * lax.rsqrt(norm))
        state[1, downs] = new_2
        n_own[t + 1, downs] = new_2.astype(jnp.bfloat16)
        downs_copy(t).start()

    last = steps - 1
    step(0, False, last > 0)
    if last > 0:
        pl.loop(1, last)(lambda t: step(t, True, True))
        step(last, True, False)
    gates_copy(last).wait_recv()
    downs_copy(last).wait_recv()
    answer(last)
    out_copy(last).start()

    def finish(t, carry):
        for copy in (key_copy, value_copy, sums_copy, gates_copy, downs_copy):
            copy(t).wait_send()
        out_copy(t).wait()
        return carry

    lax.fori_loop(0, steps, finish, 0)


def chain(steps, collective_id, queries, keys, values, counts, rate, w_first, w_third, w_second):
    slots, blocks, rows, width = queries.shape
    row_devices = lax.axis_size("rows")
    hidden = w_second.shape[1]
    half = hidden // 2
    total = slots * blocks
    flat = (total, rows, width)
    smem = pl.BlockSpec(memory_space=pltpu.SMEM)
    vmem = pl.BlockSpec(memory_space=pltpu.VMEM)
    hbm = pl.BlockSpec(memory_space=pl.ANY)
    bf16, f32 = jnp.bfloat16, jnp.float32
    return pl.pallas_call(
        functools.partial(chain_kernel, steps, slots, blocks, row_devices),
        out_shape=jax.ShapeDtypeStruct(flat, bf16),
        in_specs=[smem, smem, hbm, hbm, hbm, vmem, vmem, vmem],
        out_specs=hbm,
        scratch_shapes=[
            pltpu.VMEM(flat, bf16),
            pltpu.VMEM(flat, bf16),
            pltpu.VMEM(flat, bf16),
            pltpu.VMEM((steps, 2 * rows, width), bf16),
            pltpu.VMEM((steps, 2 * rows, width), bf16),
            pltpu.VMEM((steps + 1, 3 * half, width), bf16),
            pltpu.VMEM((steps, 3 * half, width), bf16),
            pltpu.VMEM((2, 3 * half, width), f32),
            pltpu.VMEM((steps, 8, width), f32),
            pltpu.VMEM((steps, 8, width), f32),
            pltpu.VMEM((2 * half, 1), f32),
            pltpu.VMEM((1, width), f32),
            pltpu.VMEM((steps, rows, width), bf16),
            pltpu.SemaphoreType.DMA((5,)),
            pltpu.SemaphoreType.DMA((5, steps)),
            pltpu.SemaphoreType.DMA((5, steps)),
            pltpu.SemaphoreType.DMA((steps,)),
        ],
        compiler_params=pltpu.CompilerParams(
            collective_id=collective_id, has_side_effects=True, vmem_limit_bytes=VMEM_LIMIT
        ),
        cost_estimate=pl.CostEstimate(
            flops=steps * 18 * rows * width * hidden,
            bytes_accessed=4 * 2 * total * rows * width,
            transcendentals=steps * 2 * rows * hidden,
        ),
        name="chain",
    )(
        counts, rate, queries.reshape(flat), keys.reshape(flat), values.reshape(flat),
        w_first, w_third, w_second,
    )


def place_kernel(slots, blocks, counts_ref, in_ref, out_ref, zeros, sems):
    zeros[...] = jnp.zeros_like(zeros)
    seq = lax.axis_index("seq")
    offset = jnp.int32(0)
    for slot in range(slots):
        count = counts_ref[seq * slots + slot]
        for block in range(blocks):
            at = slot * blocks + block
            source = jnp.minimum(offset + block, slots * blocks - 1)

            @pl.when(block < count)
            def _():
                pltpu.make_async_copy(in_ref.at[source], out_ref.at[at], sems.at[at]).start()

            @pl.when(block >= count)
            def _():
                pltpu.make_async_copy(zeros, out_ref.at[at], sems.at[at]).start()

        offset = offset + count
    for at in range(slots * blocks):
        pltpu.make_async_copy(zeros, out_ref.at[at], sems.at[at]).wait()


def place(slots, blocks, counts, in_order):
    return pl.pallas_call(
        functools.partial(place_kernel, slots, blocks),
        out_shape=jax.ShapeDtypeStruct(in_order.shape, in_order.dtype),
        in_specs=[pl.BlockSpec(memory_space=pltpu.SMEM), pl.BlockSpec(memory_space=pl.ANY)],
        out_specs=pl.BlockSpec(memory_space=pl.ANY),
        scratch_shapes=[
            pltpu.VMEM(in_order.shape[1:], in_order.dtype),
            pltpu.SemaphoreType.DMA((slots * blocks,)),
        ],
        compiler_params=pltpu.CompilerParams(vmem_limit_bytes=VMEM_LIMIT),
        name="place",
    )(counts, in_order)


def pair_body(queries, keys, values, counts, rate, w_first, w_third, w_second):
    slots, blocks, _, _ = queries.shape
    in_order = chain(
        slots * blocks, 0, queries, keys, values, counts, rate, w_first, w_third, w_second
    )
    return place(slots, blocks, counts, in_order).reshape(queries.shape)


def normalize_rows(matrix, epsilon):
    matrix = matrix.astype(jnp.float32)
    return matrix * lax.rsqrt(jnp.mean(matrix * matrix, axis=-1, keepdims=True) + epsilon)


def column_norms(weight):
    return jnp.sqrt(jnp.sum(weight * weight, axis=0) + 1e-06)


def rescale(moved, target):
    return moved * (target[None, :] / column_norms(moved)[None, :])


def product(first_op, second_op):
    return jnp.dot(first_op, second_op, preferred_element_type=jnp.float32)


def contract_rows(first_op, second_op):
    return lax.dot_general(
        first_op, second_op, (((0,), (0,)), ((), ())), preferred_element_type=jnp.float32
    )


def against_rows(first_op, second_op):
    return lax.dot_general(
        first_op, second_op, (((1,), (1,)), ((), ())), preferred_element_type=jnp.float32
    )


def partial_sums(current, key_rows, value_rows):
    key_norm = normalize_rows(key_rows, 1e-06).astype(jnp.bfloat16)
    gate_pre = product(key_norm, current[0])
    up_pre = product(key_norm, current[1])
    gate_sig = jax.nn.sigmoid(gate_pre)
    gate_act = gate_pre * gate_sig
    hidden = (gate_act * up_pre).astype(jnp.bfloat16)
    d_hidden = against_rows(value_rows, current[2])
    d_gate = (d_hidden * up_pre * gate_sig * (1.0 + gate_pre * (1.0 - gate_sig))).astype(
        jnp.bfloat16
    )
    d_up = (d_hidden * gate_act).astype(jnp.bfloat16)
    return (
        contract_rows(key_norm, d_gate),
        contract_rows(key_norm, d_up),
        contract_rows(hidden, value_rows),
    )


def answer(current, query_rows):
    query_norm = normalize_rows(query_rows, 1e-06).astype(jnp.bfloat16)
    out_gate = product(query_norm, current[0])
    out_up = product(query_norm, current[1])
    out_hidden = (out_gate * jax.nn.sigmoid(out_gate) * out_up).astype(jnp.bfloat16)
    return normalize_rows(product(out_hidden, current[2]), 1e-05).astype(jnp.bfloat16)


def body(queries, keys, values, counts, rate, w_first, w_third, w_second):
    seq_slots, blocks, block_rows, head_width = queries.shape
    group_index = lax.axis_index("seq")
    row_devices = lax.axis_size("rows")
    step_rate = rate[0] / (block_rows * row_devices)
    initial = (w_first[0], w_third[0], w_second[0])
    full_master = tuple((weight.astype(jnp.float32) for weight in initial))
    full_targets = tuple((column_norms(weight) for weight in full_master))

    def combine(partials):
        return (
            lax.psum(partials[0].astype(jnp.bfloat16), "rows").astype(jnp.float32),
            lax.psum(partials[1].astype(jnp.bfloat16), "rows").astype(jnp.float32),
            lax.psum(partials[2].astype(jnp.bfloat16), "rows").astype(jnp.float32),
        )

    def refresh(master):
        as_bf16 = tuple((weight.astype(jnp.bfloat16) for weight in master))
        return as_bf16

    def advance(state_pair, step_inputs):
        master, current = state_pair
        query_rows, key_rows, value_rows, restart, is_live = step_inputs
        master = tuple(
            (
                jnp.where(restart, fresh_value, kept_value)
                for fresh_value, kept_value in zip(full_master, master)
            )
        )
        current = tuple(
            (
                jnp.where(restart, fresh_value, kept_value)
                for fresh_value, kept_value in zip(initial, current)
            )
        )
        totals = combine(partial_sums(current, key_rows, value_rows))
        moved = tuple(
            (
                rescale(weight + step_rate * grad_total, target)
                for weight, grad_total, target in zip(master, totals, full_targets)
            )
        )
        master = tuple((jnp.where(is_live, new_w, old_w) for new_w, old_w in zip(moved, master)))
        current = refresh(master)
        output = answer(current, query_rows)
        return ((master, current), jnp.where(is_live, output, jnp.zeros_like(output)))

    start_pair = (full_master, initial)
    flat_shape = (seq_slots * blocks, block_rows, head_width)
    block_ids = jnp.arange(blocks, dtype=jnp.int32)
    local_counts = lax.dynamic_slice_in_dim(counts, group_index * seq_slots, seq_slots)
    restart = jnp.tile(block_ids == 0, seq_slots)
    is_live = (block_ids[None, :] < local_counts[:, None]).reshape(-1)
    inputs = (
        queries.reshape(flat_shape),
        keys.reshape(flat_shape),
        values.reshape(flat_shape),
        restart,
        is_live,
    )
    _, outputs = lax.scan(advance, start_pair, inputs)
    return outputs.reshape(queries.shape)


def any_body(queries, keys, values, counts, rate, w_first, w_third, w_second):
    pair = lax.axis_size("rows") == 2 and w_second.shape[1] % 256 == 0 and queries.shape[2] % 16 == 0
    form = pair_body if pair else body
    return form(queries, keys, values, counts, rate, w_first, w_third, w_second)


def solution(mesh):
    return jax.shard_map(
        any_body,
        mesh=mesh,
        in_specs=(
            P("seq", None, "rows", "head"),
            P("seq", None, "rows", "head"),
            P("seq", None, "rows", "head"),
            P(),
            P("head"),
            P("head", None, None),
            P("head", None, None),
            P("head", None, None),
        ),
        out_specs=P("seq", None, "rows", "head"),
        check_vma=False,
    )
```

```python
import functools

import jax
import jax.numpy as jnp
from jax import lax
from jax.experimental import pallas as pl
from jax.experimental.pallas import tpu as pltpu
from jax.sharding import PartitionSpec as P

MESH = pl.DeviceIdType.MESH
VMEM_LIMIT = 60 * 1024 * 1024


def matmul(first_op, second_op):
    return jnp.dot(first_op, second_op, preferred_element_type=jnp.float32)


def matmul_nt(first_op, second_op):
    return lax.dot_general(
        first_op, second_op, (((1,), (1,)), ((), ())), preferred_element_type=jnp.float32
    )


def unit_rows(matrix, epsilon):
    matrix = matrix.astype(jnp.float32)
    mean = jnp.mean(matrix * matrix, axis=-1, keepdims=True)
    return (matrix * lax.rsqrt(mean + epsilon)).astype(jnp.bfloat16)


def sigmoid(x):
    return 0.5 * jnp.tanh(0.5 * x) + 0.5


def chain_kernel(
    steps, slots, blocks, row_devices,
    counts_ref, rate_ref, q_hbm, k_hbm, v_hbm, w1_ref, w3_ref, w2_ref, out_ref,
    q_in, k_in, v_in, k_all, v_all, n_own, n_peer, state, sums_own, sums_peer,
    norm13, norm2, out_all, load_sem, send_sem, recv_sem, out_sem,
):
    rows = q_in.shape[1]
    half = w2_ref.shape[1] // 2
    me = lax.axis_index("rows")
    peer = {"rows": 1 - me}
    seq = lax.axis_index("seq")
    step_rate = rate_ref[0] / (rows * row_devices)
    total_blocks = slots * blocks

    def local(src, dst, at):
        return pltpu.make_async_copy(src, dst, load_sem.at[at])

    first = pl.ds(0, 1)
    rest = pl.ds(1, total_blocks - 1)
    loads = [
        local(k_hbm.at[first], k_in.at[first], 0),
        local(v_hbm.at[first], v_in.at[first], 1),
        local(k_hbm.at[rest], k_in.at[rest], 2),
        local(v_hbm.at[rest], v_in.at[rest], 3),
        local(q_hbm, q_in, 4),
    ]
    for load in loads:
        load.start()

    barrier = pltpu.get_barrier_semaphore()
    pl.semaphore_signal(barrier, inc=1, device_id=peer, device_id_type=MESH)

    def where_at(t):
        block = jnp.int32(0)
        begins = t == 0
        offset = jnp.int32(0)
        for slot in range(slots):
            begins = begins | (t == offset)
            inside = jnp.minimum(jnp.maximum(t - offset, 0), blocks - 1)
            block = jnp.where(t >= offset, slot * blocks + inside, block)
            offset = offset + counts_ref[seq * slots + slot]
        return block, begins

    def remote(src, dst, kind, t):
        return pltpu.make_async_remote_copy(
            src_ref=src, dst_ref=dst, send_sem=send_sem.at[kind, t], recv_sem=recv_sem.at[kind, t],
            device_id=peer, device_id_type=MESH,
        )

    mine, theirs = pl.ds(0, rows), pl.ds(rows, rows)
    gates, downs = pl.ds(0, 2 * half), pl.ds(2 * half, half)

    def key_copy(t):
        return remote(k_all.at[t, mine], k_all.at[t, theirs], 0, t)

    def value_copy(t):
        return remote(v_all.at[t, mine], v_all.at[t, theirs], 1, t)

    def sums_copy(t):
        return remote(sums_own.at[t], sums_peer.at[t], 2, t)

    def gates_copy(t):
        return remote(n_own.at[t + 1, gates], n_peer.at[t, gates], 3, t)

    def downs_copy(t):
        return remote(n_own.at[t + 1, downs], n_peer.at[t, downs], 4, t)

    def prepare(t, block):
        v_all[t, mine] = v_in[block]
        k_all[t, mine] = unit_rows(k_in[block], 1e-06)

    def hand_over(t):
        key_copy(t).start()
        value_copy(t).start()

    def out_copy(t):
        return pltpu.make_async_copy(out_all.at[t], out_ref.at[t], out_sem.at[t])

    units = pl.ds(pl.multiple_of(me * half, half), half)
    start_1 = w1_ref[0, :, units].astype(jnp.float32).T
    start_3 = w3_ref[0, :, units].astype(jnp.float32).T
    start_2 = w2_ref[0, units, :].astype(jnp.float32)
    start = jnp.concatenate([start_1, start_3, start_2], axis=0)
    state[0] = start
    n_own[0] = start.astype(jnp.bfloat16)
    start_13 = start[: 2 * half]
    norm13[...] = jnp.sqrt(jnp.sum(start_13 * start_13, axis=1, keepdims=True) + 1e-06)
    full_2 = w2_ref[0].astype(jnp.float32)
    norm2[...] = jnp.sqrt(jnp.sum(full_2 * full_2, axis=0, keepdims=True) + 1e-06)

    loads[0].wait()
    loads[1].wait()
    pl.semaphore_wait(barrier, 1)
    prepare(0, 0)
    hand_over(0)
    for load in loads[2:]:
        load.wait()
    if steps > 1:
        prepare(1, where_at(1)[0])
        hand_over(1)

    def answer(t):
        block, _ = where_at(t)
        query = unit_rows(q_in[block], 1e-06)
        own, other = n_own[t + 1], n_peer[t]
        hidden = []
        for weights in (own, other):
            both = matmul_nt(query, weights[: 2 * half])
            gate, up = both[:, :half], both[:, half:]
            hidden.append((gate * sigmoid(gate) * up).astype(jnp.bfloat16))
        result = matmul(
            jnp.concatenate(hidden, axis=1),
            jnp.concatenate([own[2 * half :], other[2 * half :]], axis=0),
        )
        out_all[t] = unit_rows(result, 1e-05)

    def step(t, has_before, has_after):
        _, begins = where_at(t)
        from_state = jnp.where(begins, 0, 1)
        from_n = jnp.where(begins, 0, t)
        key_copy(t).wait_recv()
        value_copy(t).wait_recv()
        if has_before:
            gates_copy(t - 2).wait_recv()
            downs_copy(t - 2).wait_recv()
        keys, values = k_all[t], v_all[t]
        both = matmul_nt(n_own[from_n, gates], keys)
        d_hidden = matmul_nt(n_own[from_n, downs], values)
        if has_after:
            prepare(t + 2, where_at(t + 2)[0])
        gate, up = both[:half], both[half:]
        sig = sigmoid(gate)
        act = gate * sig
        hidden = (act * up).astype(jnp.bfloat16)
        d_gate = (d_hidden * up * (sig + act - act * sig)).astype(jnp.bfloat16)
        d_up = (d_hidden * act).astype(jnp.bfloat16)

        moved_2 = state[from_state, downs] + step_rate * matmul(hidden, values)
        squares = moved_2 * moved_2
        sums_own[t] = jnp.sum(squares.reshape(half // 8, 8, squares.shape[1]), axis=0)
        sums_copy(t).start()
        if has_after:
            hand_over(t + 2)

        moved_13 = state[from_state, gates] + step_rate * matmul(
            jnp.concatenate([d_gate, d_up], axis=0), keys
        )
        norm = jnp.sum(moved_13 * moved_13, axis=1, keepdims=True) + 1e-06
        new_13 = moved_13 * (norm13[...] * lax.rsqrt(norm))
        state[1, gates] = new_13
        state[1, downs] = moved_2
        n_own[t + 1, gates] = new_13.astype(jnp.bfloat16)
        if has_before:
            answer(t - 2)
        gates_copy(t).start()
        if has_before:
            out_copy(t - 2).start()

        sums_copy(t).wait_recv()
        norm = jnp.sum(sums_own[t] + sums_peer[t], axis=0, keepdims=True) + 1e-06
        new_2 = state[1, downs] * (norm2[...] * lax.rsqrt(norm))
        state[1, downs] = new_2
        n_own[t + 1, downs] = new_2.astype(jnp.bfloat16)
        downs_copy(t).start()

    for t in range(min(2, steps)):
        step(t, False, t + 2 < steps)
    if steps > 4:
        pl.loop(2, steps - 2)(lambda t: step(t, True, True))
    for t in range(max(2, steps - 2), steps):
        step(t, True, False)
    for t in range(max(0, steps - 2), steps):
        gates_copy(t).wait_recv()
        downs_copy(t).wait_recv()
        answer(t)
        out_copy(t).start()

    def finish(t, carry):
        for copy in (key_copy, value_copy, sums_copy, gates_copy, downs_copy):
            copy(t).wait_send()
        out_copy(t).wait()
        return carry

    lax.fori_loop(0, steps, finish, 0)


def chain(steps, collective_id, queries, keys, values, counts, rate, w_first, w_third, w_second):
    slots, blocks, rows, width = queries.shape
    row_devices = lax.axis_size("rows")
    hidden = w_second.shape[1]
    half = hidden // 2
    total = slots * blocks
    flat = (total, rows, width)
    smem = pl.BlockSpec(memory_space=pltpu.SMEM)
    vmem = pl.BlockSpec(memory_space=pltpu.VMEM)
    hbm = pl.BlockSpec(memory_space=pl.ANY)
    bf16, f32 = jnp.bfloat16, jnp.float32
    return pl.pallas_call(
        functools.partial(chain_kernel, steps, slots, blocks, row_devices),
        out_shape=jax.ShapeDtypeStruct(flat, bf16),
        in_specs=[smem, smem, hbm, hbm, hbm, vmem, vmem, vmem],
        out_specs=hbm,
        scratch_shapes=[
            pltpu.VMEM(flat, bf16),
            pltpu.VMEM(flat, bf16),
            pltpu.VMEM(flat, bf16),
            pltpu.VMEM((steps, 2 * rows, width), bf16),
            pltpu.VMEM((steps, 2 * rows, width), bf16),
            pltpu.VMEM((steps + 1, 3 * half, width), bf16),
            pltpu.VMEM((steps, 3 * half, width), bf16),
            pltpu.VMEM((2, 3 * half, width), f32),
            pltpu.VMEM((steps, 8, width), f32),
            pltpu.VMEM((steps, 8, width), f32),
            pltpu.VMEM((2 * half, 1), f32),
            pltpu.VMEM((1, width), f32),
            pltpu.VMEM((steps, rows, width), bf16),
            pltpu.SemaphoreType.DMA((5,)),
            pltpu.SemaphoreType.DMA((5, steps)),
            pltpu.SemaphoreType.DMA((5, steps)),
            pltpu.SemaphoreType.DMA((steps,)),
        ],
        compiler_params=pltpu.CompilerParams(
            collective_id=collective_id, has_side_effects=True, vmem_limit_bytes=VMEM_LIMIT
        ),
        cost_estimate=pl.CostEstimate(
            flops=steps * 18 * rows * width * hidden,
            bytes_accessed=4 * 2 * total * rows * width,
            transcendentals=steps * 2 * rows * hidden,
        ),
        name="chain",
    )(
        counts, rate, queries.reshape(flat), keys.reshape(flat), values.reshape(flat),
        w_first, w_third, w_second,
    )


def place_kernel(slots, blocks, counts_ref, in_ref, out_ref, held, in_sems, out_sems):
    seq = lax.axis_index("seq")
    total = slots * blocks

    def load(at, source):
        return pltpu.make_async_copy(in_ref.at[source], held.at[at], in_sems.at[at])

    def store(at):
        return pltpu.make_async_copy(held.at[at], out_ref.at[at], out_sems.at[at])

    live = []
    offset = jnp.int32(0)
    for slot in range(slots):
        count = counts_ref[seq * slots + slot]
        for block in range(blocks):
            at = slot * blocks + block
            live.append(block < count)
            source = jnp.minimum(offset + block, total - 1)
            pl.when(live[at])(lambda: load(at, source).start())
        offset = offset + count
    for at in range(total):

        @pl.when(jnp.logical_not(live[at]))
        def _():
            held[at] = jnp.zeros(held.shape[1:], held.dtype)
            store(at).start()

    for at in range(total):

        @pl.when(live[at])
        def _():
            load(at, 0).wait()
            store(at).start()

    for at in range(total):
        store(at).wait()


def place(slots, blocks, counts, in_order):
    return pl.pallas_call(
        functools.partial(place_kernel, slots, blocks),
        out_shape=jax.ShapeDtypeStruct(in_order.shape, in_order.dtype),
        in_specs=[pl.BlockSpec(memory_space=pltpu.SMEM), pl.BlockSpec(memory_space=pl.ANY)],
        out_specs=pl.BlockSpec(memory_space=pl.ANY),
        scratch_shapes=[
            pltpu.VMEM(in_order.shape, in_order.dtype),
            pltpu.SemaphoreType.DMA((slots * blocks,)),
            pltpu.SemaphoreType.DMA((slots * blocks,)),
        ],
        compiler_params=pltpu.CompilerParams(vmem_limit_bytes=VMEM_LIMIT),
        name="place",
    )(counts, in_order)


def pair_body(queries, keys, values, counts, rate, w_first, w_third, w_second):
    slots, blocks, _, _ = queries.shape
    in_order = chain(
        slots * blocks, 0, queries, keys, values, counts, rate, w_first, w_third, w_second
    )
    return place(slots, blocks, counts, in_order).reshape(queries.shape)


def normalize_rows(matrix, epsilon):
    matrix = matrix.astype(jnp.float32)
    return matrix * lax.rsqrt(jnp.mean(matrix * matrix, axis=-1, keepdims=True) + epsilon)


def column_norms(weight):
    return jnp.sqrt(jnp.sum(weight * weight, axis=0) + 1e-06)


def rescale(moved, target):
    return moved * (target[None, :] / column_norms(moved)[None, :])


def product(first_op, second_op):
    return jnp.dot(first_op, second_op, preferred_element_type=jnp.float32)


def contract_rows(first_op, second_op):
    return lax.dot_general(
        first_op, second_op, (((0,), (0,)), ((), ())), preferred_element_type=jnp.float32
    )


def against_rows(first_op, second_op):
    return lax.dot_general(
        first_op, second_op, (((1,), (1,)), ((), ())), preferred_element_type=jnp.float32
    )


def partial_sums(current, key_rows, value_rows):
    key_norm = normalize_rows(key_rows, 1e-06).astype(jnp.bfloat16)
    gate_pre = product(key_norm, current[0])
    up_pre = product(key_norm, current[1])
    gate_sig = jax.nn.sigmoid(gate_pre)
    gate_act = gate_pre * gate_sig
    hidden = (gate_act * up_pre).astype(jnp.bfloat16)
    d_hidden = against_rows(value_rows, current[2])
    d_gate = (d_hidden * up_pre * gate_sig * (1.0 + gate_pre * (1.0 - gate_sig))).astype(
        jnp.bfloat16
    )
    d_up = (d_hidden * gate_act).astype(jnp.bfloat16)
    return (
        contract_rows(key_norm, d_gate),
        contract_rows(key_norm, d_up),
        contract_rows(hidden, value_rows),
    )


def answer(current, query_rows):
    query_norm = normalize_rows(query_rows, 1e-06).astype(jnp.bfloat16)
    out_gate = product(query_norm, current[0])
    out_up = product(query_norm, current[1])
    out_hidden = (out_gate * jax.nn.sigmoid(out_gate) * out_up).astype(jnp.bfloat16)
    return normalize_rows(product(out_hidden, current[2]), 1e-05).astype(jnp.bfloat16)


def body(queries, keys, values, counts, rate, w_first, w_third, w_second):
    seq_slots, blocks, block_rows, head_width = queries.shape
    group_index = lax.axis_index("seq")
    row_devices = lax.axis_size("rows")
    step_rate = rate[0] / (block_rows * row_devices)
    initial = (w_first[0], w_third[0], w_second[0])
    full_master = tuple((weight.astype(jnp.float32) for weight in initial))
    full_targets = tuple((column_norms(weight) for weight in full_master))

    def combine(partials):
        return (
            lax.psum(partials[0].astype(jnp.bfloat16), "rows").astype(jnp.float32),
            lax.psum(partials[1].astype(jnp.bfloat16), "rows").astype(jnp.float32),
            lax.psum(partials[2].astype(jnp.bfloat16), "rows").astype(jnp.float32),
        )

    def refresh(master):
        as_bf16 = tuple((weight.astype(jnp.bfloat16) for weight in master))
        return as_bf16

    def advance(state_pair, step_inputs):
        master, current = state_pair
        query_rows, key_rows, value_rows, restart, is_live = step_inputs
        master = tuple(
            (
                jnp.where(restart, fresh_value, kept_value)
                for fresh_value, kept_value in zip(full_master, master)
            )
        )
        current = tuple(
            (
                jnp.where(restart, fresh_value, kept_value)
                for fresh_value, kept_value in zip(initial, current)
            )
        )
        totals = combine(partial_sums(current, key_rows, value_rows))
        moved = tuple(
            (
                rescale(weight + step_rate * grad_total, target)
                for weight, grad_total, target in zip(master, totals, full_targets)
            )
        )
        master = tuple((jnp.where(is_live, new_w, old_w) for new_w, old_w in zip(moved, master)))
        current = refresh(master)
        output = answer(current, query_rows)
        return ((master, current), jnp.where(is_live, output, jnp.zeros_like(output)))

    start_pair = (full_master, initial)
    flat_shape = (seq_slots * blocks, block_rows, head_width)
    block_ids = jnp.arange(blocks, dtype=jnp.int32)
    local_counts = lax.dynamic_slice_in_dim(counts, group_index * seq_slots, seq_slots)
    restart = jnp.tile(block_ids == 0, seq_slots)
    is_live = (block_ids[None, :] < local_counts[:, None]).reshape(-1)
    inputs = (
        queries.reshape(flat_shape),
        keys.reshape(flat_shape),
        values.reshape(flat_shape),
        restart,
        is_live,
    )
    _, outputs = lax.scan(advance, start_pair, inputs)
    return outputs.reshape(queries.shape)


def any_body(queries, keys, values, counts, rate, w_first, w_third, w_second):
    pair = lax.axis_size("rows") == 2 and w_second.shape[1] % 256 == 0 and queries.shape[2] % 16 == 0
    form = pair_body if pair else body
    return form(queries, keys, values, counts, rate, w_first, w_third, w_second)


def solution(mesh):
    return jax.shard_map(
        any_body,
        mesh=mesh,
        in_specs=(
            P("seq", None, "rows", "head"),
            P("seq", None, "rows", "head"),
            P("seq", None, "rows", "head"),
            P(),
            P("head"),
            P("head", None, None),
            P("head", None, None),
            P("head", None, None),
        ),
        out_specs=P("seq", None, "rows", "head"),
        check_vma=False,
    )
```

```python
import functools

import jax
import jax.numpy as jnp
from jax import lax
from jax.experimental import pallas as pl
from jax.experimental.pallas import tpu as pltpu
from jax.sharding import PartitionSpec as P

MESH = pl.DeviceIdType.MESH
VMEM_LIMIT = 60 * 1024 * 1024


def matmul(first_op, second_op):
    return jnp.dot(first_op, second_op, preferred_element_type=jnp.float32)


def matmul_nt(first_op, second_op):
    return lax.dot_general(
        first_op, second_op, (((1,), (1,)), ((), ())), preferred_element_type=jnp.float32
    )


def unit_rows(matrix, epsilon):
    matrix = matrix.astype(jnp.float32)
    mean = jnp.mean(matrix * matrix, axis=-1, keepdims=True)
    return (matrix * lax.rsqrt(mean + epsilon)).astype(jnp.bfloat16)


def sigmoid(x):
    return 0.5 * jnp.tanh(0.5 * x) + 0.5


def chain_kernel(
    steps, slots, blocks, row_devices,
    counts_ref, rate_ref, q_hbm, k_hbm, v_hbm, w1_ref, w3_ref, w2_ref, out_ref,
    q_in, k_in, v_in, k_all, v_all, n_own, n_peer, state, sums_own, sums_peer,
    norm13, norm2, out_all, load_sem, send_sem, recv_sem, out_sem,
):
    rows = q_in.shape[1]
    half = w2_ref.shape[1] // 2
    me = lax.axis_index("rows")
    peer = {"rows": 1 - me}
    seq = lax.axis_index("seq")
    step_rate = rate_ref[0] / (rows * row_devices)
    total_blocks = slots * blocks

    def local(src, dst, at):
        return pltpu.make_async_copy(src, dst, load_sem.at[at])

    first = pl.ds(0, 1)
    rest = pl.ds(1, total_blocks - 1)
    loads = [
        local(k_hbm.at[first], k_in.at[first], 0),
        local(v_hbm.at[first], v_in.at[first], 1),
        local(k_hbm.at[rest], k_in.at[rest], 2),
        local(v_hbm.at[rest], v_in.at[rest], 3),
        local(q_hbm, q_in, 4),
    ]
    for load in loads:
        load.start()

    barrier = pltpu.get_barrier_semaphore()
    pl.semaphore_signal(barrier, inc=1, device_id=peer, device_id_type=MESH)

    def where_at(t):
        block = jnp.int32(0)
        begins = t == 0
        offset = jnp.int32(0)
        for slot in range(slots):
            begins = begins | (t == offset)
            inside = jnp.minimum(jnp.maximum(t - offset, 0), blocks - 1)
            block = jnp.where(t >= offset, slot * blocks + inside, block)
            offset = offset + counts_ref[seq * slots + slot]
        return block, begins

    def remote(src, dst, kind, t):
        return pltpu.make_async_remote_copy(
            src_ref=src, dst_ref=dst, send_sem=send_sem.at[kind, t], recv_sem=recv_sem.at[kind, t],
            device_id=peer, device_id_type=MESH,
        )

    mine, theirs = pl.ds(0, rows), pl.ds(rows, rows)
    gates, downs = pl.ds(0, 2 * half), pl.ds(2 * half, half)

    def key_copy(t):
        return remote(k_all.at[t, mine], k_all.at[t, theirs], 0, t)

    def value_copy(t):
        return remote(v_all.at[t, mine], v_all.at[t, theirs], 1, t)

    def sums_copy(t):
        return remote(sums_own.at[t], sums_peer.at[t], 2, t)

    def gates_copy(t):
        return remote(n_own.at[t + 1, gates], n_peer.at[t, gates], 3, t)

    def downs_copy(t):
        return remote(n_own.at[t + 1, downs], n_peer.at[t, downs], 4, t)

    def prepare(t, block):
        v_all[t, mine] = v_in[block]
        k_all[t, mine] = unit_rows(k_in[block], 1e-06)

    def hand_over(t):
        key_copy(t).start()
        value_copy(t).start()

    def out_copy(t):
        return pltpu.make_async_copy(out_all.at[t], out_ref.at[t], out_sem.at[t])

    units = pl.ds(pl.multiple_of(me * half, half), half)
    start_1 = w1_ref[0, :, units].astype(jnp.float32).T
    start_3 = w3_ref[0, :, units].astype(jnp.float32).T
    start_2 = w2_ref[0, units, :].astype(jnp.float32)
    start = jnp.concatenate([start_1, start_3, start_2], axis=0)
    state[0] = start
    n_own[0] = start.astype(jnp.bfloat16)
    start_13 = start[: 2 * half]
    norm13[...] = jnp.sqrt(jnp.sum(start_13 * start_13, axis=1, keepdims=True) + 1e-06)
    full_2 = w2_ref[0].astype(jnp.float32)
    norm2[...] = jnp.sqrt(jnp.sum(full_2 * full_2, axis=0, keepdims=True) + 1e-06)

    loads[0].wait()
    loads[1].wait()
    pl.semaphore_wait(barrier, 1)
    prepare(0, 0)
    hand_over(0)
    for load in loads[2:]:
        load.wait()
    if steps > 1:
        prepare(1, where_at(1)[0])
        hand_over(1)

    def answer(t):
        block, _ = where_at(t)
        query = unit_rows(q_in[block], 1e-06)
        own, other = n_own[t + 1], n_peer[t]
        hidden = []
        for weights in (own, other):
            both = matmul_nt(query, weights[: 2 * half])
            gate, up = both[:, :half], both[:, half:]
            hidden.append((gate * sigmoid(gate) * up).astype(jnp.bfloat16))
        result = matmul(
            jnp.concatenate(hidden, axis=1),
            jnp.concatenate([own[2 * half :], other[2 * half :]], axis=0),
        )
        out_all[t] = unit_rows(result, 1e-05)

    def step(t, has_before, has_after):
        _, begins = where_at(t)
        from_state = jnp.where(begins, 0, 1)
        from_n = jnp.where(begins, 0, t)
        key_copy(t).wait_recv()
        value_copy(t).wait_recv()
        if has_before:
            gates_copy(t - 2).wait_recv()
            downs_copy(t - 2).wait_recv()
        keys, values = k_all[t], v_all[t]
        both = matmul_nt(n_own[from_n, gates], keys)
        d_hidden = matmul_nt(n_own[from_n, downs], values)
        if has_after:
            prepare(t + 2, where_at(t + 2)[0])
        gate, up = both[:half], both[half:]
        sig = sigmoid(gate)
        act = gate * sig
        hidden = (act * up).astype(jnp.bfloat16)
        d_gate = (d_hidden * up * (sig + act - act * sig)).astype(jnp.bfloat16)
        d_up = (d_hidden * act).astype(jnp.bfloat16)

        moved_2 = state[from_state, downs] + step_rate * matmul(hidden, values)
        squares = moved_2 * moved_2
        sums_own[t] = jnp.sum(squares.reshape(half // 8, 8, squares.shape[1]), axis=0)
        sums_copy(t).start()
        if has_after:
            hand_over(t + 2)

        moved_13 = state[from_state, gates] + step_rate * matmul(
            jnp.concatenate([d_gate, d_up], axis=0), keys
        )
        norm = jnp.sum(moved_13 * moved_13, axis=1, keepdims=True) + 1e-06
        new_13 = moved_13 * (norm13[...] * lax.rsqrt(norm))
        state[1, gates] = new_13
        state[1, downs] = moved_2
        n_own[t + 1, gates] = new_13.astype(jnp.bfloat16)
        if has_before:
            answer(t - 2)
        gates_copy(t).start()
        if has_before:
            out_copy(t - 2).start()

        sums_copy(t).wait_recv()
        norm = jnp.sum(sums_own[t] + sums_peer[t], axis=0, keepdims=True) + 1e-06
        new_2 = state[1, downs] * (norm2[...] * lax.rsqrt(norm))
        state[1, downs] = new_2
        n_own[t + 1, downs] = new_2.astype(jnp.bfloat16)
        downs_copy(t).start()

    for t in range(min(2, steps)):
        step(t, False, t + 2 < steps)
    if steps > 4:
        pl.loop(2, steps - 2)(lambda t: step(t, True, True))
    for t in range(max(2, steps - 2), steps):
        step(t, True, False)
    for t in range(max(0, steps - 2), steps):
        gates_copy(t).wait_recv()
        downs_copy(t).wait_recv()
        answer(t)
        out_copy(t).start()

    def finish(t, carry):
        for copy in (key_copy, value_copy, sums_copy, gates_copy, downs_copy):
            copy(t).wait_send()
        out_copy(t).wait()
        return carry

    lax.fori_loop(0, steps, finish, 0)


def chain(steps, collective_id, queries, keys, values, counts, rate, w_first, w_third, w_second):
    slots, blocks, rows, width = queries.shape
    row_devices = lax.axis_size("rows")
    hidden = w_second.shape[1]
    half = hidden // 2
    total = slots * blocks
    flat = (total, rows, width)
    smem = pl.BlockSpec(memory_space=pltpu.SMEM)
    vmem = pl.BlockSpec(memory_space=pltpu.VMEM)
    hbm = pl.BlockSpec(memory_space=pl.ANY)
    bf16, f32 = jnp.bfloat16, jnp.float32
    return pl.pallas_call(
        functools.partial(chain_kernel, steps, slots, blocks, row_devices),
        out_shape=jax.ShapeDtypeStruct(flat, bf16),
        in_specs=[smem, smem, hbm, hbm, hbm, vmem, vmem, vmem],
        out_specs=hbm,
        scratch_shapes=[
            pltpu.VMEM(flat, bf16),
            pltpu.VMEM(flat, bf16),
            pltpu.VMEM(flat, bf16),
            pltpu.VMEM((steps, 2 * rows, width), bf16),
            pltpu.VMEM((steps, 2 * rows, width), bf16),
            pltpu.VMEM((steps + 1, 3 * half, width), bf16),
            pltpu.VMEM((steps, 3 * half, width), bf16),
            pltpu.VMEM((2, 3 * half, width), f32),
            pltpu.VMEM((steps, 8, width), f32),
            pltpu.VMEM((steps, 8, width), f32),
            pltpu.VMEM((2 * half, 1), f32),
            pltpu.VMEM((1, width), f32),
            pltpu.VMEM((steps, rows, width), bf16),
            pltpu.SemaphoreType.DMA((5,)),
            pltpu.SemaphoreType.DMA((5, steps)),
            pltpu.SemaphoreType.DMA((5, steps)),
            pltpu.SemaphoreType.DMA((steps,)),
        ],
        compiler_params=pltpu.CompilerParams(
            collective_id=collective_id, has_side_effects=True, vmem_limit_bytes=VMEM_LIMIT
        ),
        cost_estimate=pl.CostEstimate(
            flops=steps * 18 * rows * width * hidden,
            bytes_accessed=4 * 2 * total * rows * width,
            transcendentals=steps * 2 * rows * hidden,
        ),
        name="chain",
    )(
        counts, rate, queries.reshape(flat), keys.reshape(flat), values.reshape(flat),
        w_first, w_third, w_second,
    )


def place_kernel(slots, blocks, counts_ref, in_ref, out_ref, held, in_sems, out_sems):
    seq = lax.axis_index("seq")
    total = slots * blocks

    def load(at, source):
        return pltpu.make_async_copy(in_ref.at[source], held.at[at], in_sems.at[at])

    def store(at):
        return pltpu.make_async_copy(held.at[at], out_ref.at[at], out_sems.at[at])

    live = []
    offset = jnp.int32(0)
    for slot in range(slots):
        count = counts_ref[seq * slots + slot]
        for block in range(blocks):
            at = slot * blocks + block
            live.append(block < count)
            source = jnp.minimum(offset + block, total - 1)
            pl.when(live[at])(lambda: load(at, source).start())
        offset = offset + count
    for at in range(total):

        @pl.when(jnp.logical_not(live[at]))
        def _():
            held[at] = jnp.zeros(held.shape[1:], held.dtype)
            store(at).start()

    for at in range(total):

        @pl.when(live[at])
        def _():
            load(at, 0).wait()
            store(at).start()

    for at in range(total):
        store(at).wait()


def place(slots, blocks, counts, in_order):
    return pl.pallas_call(
        functools.partial(place_kernel, slots, blocks),
        out_shape=jax.ShapeDtypeStruct(in_order.shape, in_order.dtype),
        in_specs=[pl.BlockSpec(memory_space=pltpu.SMEM), pl.BlockSpec(memory_space=pl.ANY)],
        out_specs=pl.BlockSpec(memory_space=pl.ANY),
        scratch_shapes=[
            pltpu.VMEM(in_order.shape, in_order.dtype),
            pltpu.SemaphoreType.DMA((slots * blocks,)),
            pltpu.SemaphoreType.DMA((slots * blocks,)),
        ],
        compiler_params=pltpu.CompilerParams(vmem_limit_bytes=VMEM_LIMIT),
        name="place",
    )(counts, in_order)


def pair_body(queries, keys, values, counts, rate, w_first, w_third, w_second):
    slots, blocks, _, _ = queries.shape
    fewest, most = blocks + slots - 1, slots * blocks
    longest = jnp.max(jnp.sum(counts.reshape(-1, slots), axis=1))
    forms = [functools.partial(chain, steps, steps - fewest) for steps in range(fewest, most + 1)]
    in_order = lax.switch(
        longest - fewest, forms, queries, keys, values, counts, rate, w_first, w_third, w_second
    )
    return place(slots, blocks, counts, in_order).reshape(queries.shape)


def normalize_rows(matrix, epsilon):
    matrix = matrix.astype(jnp.float32)
    return matrix * lax.rsqrt(jnp.mean(matrix * matrix, axis=-1, keepdims=True) + epsilon)


def column_norms(weight):
    return jnp.sqrt(jnp.sum(weight * weight, axis=0) + 1e-06)


def rescale(moved, target):
    return moved * (target[None, :] / column_norms(moved)[None, :])


def product(first_op, second_op):
    return jnp.dot(first_op, second_op, preferred_element_type=jnp.float32)


def contract_rows(first_op, second_op):
    return lax.dot_general(
        first_op, second_op, (((0,), (0,)), ((), ())), preferred_element_type=jnp.float32
    )


def against_rows(first_op, second_op):
    return lax.dot_general(
        first_op, second_op, (((1,), (1,)), ((), ())), preferred_element_type=jnp.float32
    )


def partial_sums(current, key_rows, value_rows):
    key_norm = normalize_rows(key_rows, 1e-06).astype(jnp.bfloat16)
    gate_pre = product(key_norm, current[0])
    up_pre = product(key_norm, current[1])
    gate_sig = jax.nn.sigmoid(gate_pre)
    gate_act = gate_pre * gate_sig
    hidden = (gate_act * up_pre).astype(jnp.bfloat16)
    d_hidden = against_rows(value_rows, current[2])
    d_gate = (d_hidden * up_pre * gate_sig * (1.0 + gate_pre * (1.0 - gate_sig))).astype(
        jnp.bfloat16
    )
    d_up = (d_hidden * gate_act).astype(jnp.bfloat16)
    return (
        contract_rows(key_norm, d_gate),
        contract_rows(key_norm, d_up),
        contract_rows(hidden, value_rows),
    )


def answer(current, query_rows):
    query_norm = normalize_rows(query_rows, 1e-06).astype(jnp.bfloat16)
    out_gate = product(query_norm, current[0])
    out_up = product(query_norm, current[1])
    out_hidden = (out_gate * jax.nn.sigmoid(out_gate) * out_up).astype(jnp.bfloat16)
    return normalize_rows(product(out_hidden, current[2]), 1e-05).astype(jnp.bfloat16)


def body(queries, keys, values, counts, rate, w_first, w_third, w_second):
    seq_slots, blocks, block_rows, head_width = queries.shape
    group_index = lax.axis_index("seq")
    row_devices = lax.axis_size("rows")
    step_rate = rate[0] / (block_rows * row_devices)
    initial = (w_first[0], w_third[0], w_second[0])
    full_master = tuple((weight.astype(jnp.float32) for weight in initial))
    full_targets = tuple((column_norms(weight) for weight in full_master))

    def combine(partials):
        return (
            lax.psum(partials[0].astype(jnp.bfloat16), "rows").astype(jnp.float32),
            lax.psum(partials[1].astype(jnp.bfloat16), "rows").astype(jnp.float32),
            lax.psum(partials[2].astype(jnp.bfloat16), "rows").astype(jnp.float32),
        )

    def refresh(master):
        as_bf16 = tuple((weight.astype(jnp.bfloat16) for weight in master))
        return as_bf16

    def advance(state_pair, step_inputs):
        master, current = state_pair
        query_rows, key_rows, value_rows, restart, is_live = step_inputs
        master = tuple(
            (
                jnp.where(restart, fresh_value, kept_value)
                for fresh_value, kept_value in zip(full_master, master)
            )
        )
        current = tuple(
            (
                jnp.where(restart, fresh_value, kept_value)
                for fresh_value, kept_value in zip(initial, current)
            )
        )
        totals = combine(partial_sums(current, key_rows, value_rows))
        moved = tuple(
            (
                rescale(weight + step_rate * grad_total, target)
                for weight, grad_total, target in zip(master, totals, full_targets)
            )
        )
        master = tuple((jnp.where(is_live, new_w, old_w) for new_w, old_w in zip(moved, master)))
        current = refresh(master)
        output = answer(current, query_rows)
        return ((master, current), jnp.where(is_live, output, jnp.zeros_like(output)))

    start_pair = (full_master, initial)
    flat_shape = (seq_slots * blocks, block_rows, head_width)
    block_ids = jnp.arange(blocks, dtype=jnp.int32)
    local_counts = lax.dynamic_slice_in_dim(counts, group_index * seq_slots, seq_slots)
    restart = jnp.tile(block_ids == 0, seq_slots)
    is_live = (block_ids[None, :] < local_counts[:, None]).reshape(-1)
    inputs = (
        queries.reshape(flat_shape),
        keys.reshape(flat_shape),
        values.reshape(flat_shape),
        restart,
        is_live,
    )
    _, outputs = lax.scan(advance, start_pair, inputs)
    return outputs.reshape(queries.shape)


def any_body(queries, keys, values, counts, rate, w_first, w_third, w_second):
    pair = lax.axis_size("rows") == 2 and w_second.shape[1] % 256 == 0 and queries.shape[2] % 16 == 0
    form = pair_body if pair else body
    return form(queries, keys, values, counts, rate, w_first, w_third, w_second)


def solution(mesh):
    return jax.shard_map(
        any_body,
        mesh=mesh,
        in_specs=(
            P("seq", None, "rows", "head"),
            P("seq", None, "rows", "head"),
            P("seq", None, "rows", "head"),
            P(),
            P("head"),
            P("head", None, None),
            P("head", None, None),
            P("head", None, None),
        ),
        out_specs=P("seq", None, "rows", "head"),
        check_vma=False,
    )
```

```python
import functools

import jax
import jax.numpy as jnp
from jax import lax
from jax.experimental import pallas as pl
from jax.experimental.pallas import tpu as pltpu
from jax.sharding import PartitionSpec as P

MESH = pl.DeviceIdType.MESH
VMEM_LIMIT = 60 * 1024 * 1024


def matmul(first_op, second_op):
    return jnp.dot(first_op, second_op, preferred_element_type=jnp.float32)


def matmul_nt(first_op, second_op):
    return lax.dot_general(
        first_op, second_op, (((1,), (1,)), ((), ())), preferred_element_type=jnp.float32
    )


def unit_rows(matrix, epsilon):
    matrix = matrix.astype(jnp.float32)
    mean = jnp.mean(matrix * matrix, axis=-1, keepdims=True)
    return (matrix * lax.rsqrt(mean + epsilon)).astype(jnp.bfloat16)


def sigmoid(x):
    return 0.5 * jnp.tanh(0.5 * x) + 0.5


def chain_kernel(
    steps, slots, blocks, row_devices,
    counts_ref, rate_ref, q_hbm, k_hbm, v_hbm, w1_hbm, w3_hbm, w2_hbm, out_ref,
    q_in, k_in, v_in, k_all, v_all, n_own, n_peer, state, sums_own, sums_peer,
    norm13, norm2, out_all, w1_ref, w3_ref, w2_ref, load_sem, send_sem, recv_sem, out_sem,
):
    rows = q_in.shape[1]
    half = w2_ref.shape[1] // 2
    me = lax.axis_index("rows")
    peer = {"rows": 1 - me}
    seq = lax.axis_index("seq")
    step_rate = rate_ref[0] / (rows * row_devices)
    total_blocks = slots * blocks

    def local(src, dst, at):
        return pltpu.make_async_copy(src, dst, load_sem.at[at])

    first = pl.ds(0, 1)
    rest = pl.ds(1, total_blocks - 1)
    loads = [
        local(k_hbm.at[first], k_in.at[first], 0),
        local(v_hbm.at[first], v_in.at[first], 1),
        local(k_hbm.at[rest], k_in.at[rest], 2),
        local(v_hbm.at[rest], v_in.at[rest], 3),
        local(q_hbm, q_in, 4),
    ]
    weight_loads = [
        local(w1_hbm, w1_ref, 5),
        local(w3_hbm, w3_ref, 6),
        local(w2_hbm, w2_ref, 7),
    ]
    for load in loads[:2] + weight_loads:
        load.start()

    barrier = pltpu.get_barrier_semaphore()
    pl.semaphore_signal(barrier, inc=1, device_id=peer, device_id_type=MESH)

    def where_at(t):
        block = jnp.int32(0)
        begins = t == 0
        offset = jnp.int32(0)
        for slot in range(slots):
            begins = begins | (t == offset)
            inside = jnp.minimum(jnp.maximum(t - offset, 0), blocks - 1)
            block = jnp.where(t >= offset, slot * blocks + inside, block)
            offset = offset + counts_ref[seq * slots + slot]
        return block, begins

    def remote(src, dst, kind, t):
        return pltpu.make_async_remote_copy(
            src_ref=src, dst_ref=dst, send_sem=send_sem.at[kind, t], recv_sem=recv_sem.at[kind, t],
            device_id=peer, device_id_type=MESH,
        )

    mine, theirs = pl.ds(0, rows), pl.ds(rows, rows)
    gates, downs = pl.ds(0, 2 * half), pl.ds(2 * half, half)

    def key_copy(t):
        return remote(k_all.at[t, mine], k_all.at[t, theirs], 0, t)

    def value_copy(t):
        return remote(v_all.at[t, mine], v_all.at[t, theirs], 1, t)

    def sums_copy(t):
        return remote(sums_own.at[t], sums_peer.at[t], 2, t)

    def gates_copy(t):
        return remote(n_own.at[t + 1, gates], n_peer.at[t, gates], 3, t)

    def downs_copy(t):
        return remote(n_own.at[t + 1, downs], n_peer.at[t, downs], 4, t)

    def prepare(t, block):
        v_all[t, mine] = v_in[block]
        k_all[t, mine] = unit_rows(k_in[block], 1e-06)

    def hand_over(t):
        key_copy(t).start()
        value_copy(t).start()

    def out_copy(t):
        return pltpu.make_async_copy(out_all.at[t], out_ref.at[t], out_sem.at[t])

    pl.semaphore_wait(barrier, 1)
    loads[0].wait()
    k_all[0, mine] = unit_rows(k_in[0], 1e-06)
    key_copy(0).start()
    loads[1].wait()
    v_all[0, mine] = v_in[0]
    value_copy(0).start()
    for load in loads[2:4]:
        load.start()
    for load in weight_loads:
        load.wait()

    units = pl.ds(pl.multiple_of(me * half, half), half)
    start_1 = w1_ref[0, :, units].astype(jnp.float32).T
    start_3 = w3_ref[0, :, units].astype(jnp.float32).T
    start_2 = w2_ref[0, units, :].astype(jnp.float32)
    start = jnp.concatenate([start_1, start_3, start_2], axis=0)
    state[0] = start
    n_own[0] = start.astype(jnp.bfloat16)
    start_13 = start[: 2 * half]
    norm13[...] = jnp.sqrt(jnp.sum(start_13 * start_13, axis=1, keepdims=True) + 1e-06)
    full_2 = w2_ref[0].astype(jnp.float32)
    norm2[...] = jnp.sqrt(jnp.sum(full_2 * full_2, axis=0, keepdims=True) + 1e-06)

    def answer(t):
        block, _ = where_at(t)
        query = unit_rows(q_in[block], 1e-06)
        own, other = n_own[t + 1], n_peer[t]
        hidden = []
        for weights in (own, other):
            both = matmul_nt(query, weights[: 2 * half])
            gate, up = both[:, :half], both[:, half:]
            hidden.append((gate * sigmoid(gate) * up).astype(jnp.bfloat16))
        result = matmul(
            jnp.concatenate(hidden, axis=1),
            jnp.concatenate([own[2 * half :], other[2 * half :]], axis=0),
        )
        out_all[t] = unit_rows(result, 1e-05)

    def step(t, has_before, has_after):
        _, begins = where_at(t)
        from_state = jnp.where(begins, 0, 1)
        from_n = jnp.where(begins, 0, t)
        first_step = not has_before and t == 0
        if has_before:
            gates_copy(t - 2).wait_recv()
            downs_copy(t - 2).wait_recv()
        moved_2 = state[from_state, downs]
        moved_13 = state[from_state, gates]
        for part in (mine, theirs) if first_step else (pl.ds(0, 2 * rows),):
            if part is not mine:
                key_copy(t).wait_recv()
                value_copy(t).wait_recv()
            keys, values = k_all[t, part], v_all[t, part]
            both = matmul_nt(n_own[from_n, gates], keys)
            d_hidden = matmul_nt(n_own[from_n, downs], values)
            if has_after and not first_step:
                prepare(t + 2, where_at(t + 2)[0])
            gate, up = both[:half], both[half:]
            sig = sigmoid(gate)
            act = gate * sig
            hidden = (act * up).astype(jnp.bfloat16)
            d_gate = (d_hidden * up * (sig + act - act * sig)).astype(jnp.bfloat16)
            d_up = (d_hidden * act).astype(jnp.bfloat16)
            moved_2 = moved_2 + step_rate * matmul(hidden, values)
            if part is mine:
                moved_13 = moved_13 + step_rate * matmul(
                    jnp.concatenate([d_gate, d_up], axis=0), keys
                )
                for load in loads[2:4]:
                    load.wait()
                loads[4].start()
                for later in range(1, min(3, steps)):
                    prepare(later, where_at(later)[0])
                    hand_over(later)

        squares = moved_2 * moved_2
        sums_own[t] = jnp.sum(squares.reshape(half // 8, 8, squares.shape[1]), axis=0)
        sums_copy(t).start()
        if has_after and not first_step:
            hand_over(t + 2)

        moved_13 = moved_13 + step_rate * matmul(jnp.concatenate([d_gate, d_up], axis=0), keys)
        norm = jnp.sum(moved_13 * moved_13, axis=1, keepdims=True) + 1e-06
        new_13 = moved_13 * (norm13[...] * lax.rsqrt(norm))
        state[1, gates] = new_13
        state[1, downs] = moved_2
        n_own[t + 1, gates] = new_13.astype(jnp.bfloat16)
        if has_before:
            answer(t - 2)
        gates_copy(t).start()
        if has_before:
            out_copy(t - 2).start()

        sums_copy(t).wait_recv()
        norm = jnp.sum(sums_own[t] + sums_peer[t], axis=0, keepdims=True) + 1e-06
        new_2 = state[1, downs] * (norm2[...] * lax.rsqrt(norm))
        state[1, downs] = new_2
        n_own[t + 1, downs] = new_2.astype(jnp.bfloat16)
        downs_copy(t).start()

    for t in range(min(2, steps)):
        step(t, False, t + 2 < steps)
    loads[4].wait()
    if steps > 4:
        pl.loop(2, steps - 2)(lambda t: step(t, True, True))
    for t in range(max(2, steps - 2), steps):
        step(t, True, False)
    for t in range(max(0, steps - 2), steps):
        gates_copy(t).wait_recv()
        downs_copy(t).wait_recv()
        answer(t)
        out_copy(t).start()

    def finish(t, carry):
        for copy in (key_copy, value_copy, sums_copy, gates_copy, downs_copy):
            copy(t).wait_send()
        out_copy(t).wait()
        return carry

    lax.fori_loop(0, steps, finish, 0)


def chain(steps, collective_id, queries, keys, values, counts, rate, w_first, w_third, w_second):
    slots, blocks, rows, width = queries.shape
    row_devices = lax.axis_size("rows")
    hidden = w_second.shape[1]
    half = hidden // 2
    total = slots * blocks
    flat = (total, rows, width)
    smem = pl.BlockSpec(memory_space=pltpu.SMEM)
    hbm = pl.BlockSpec(memory_space=pl.ANY)
    bf16, f32 = jnp.bfloat16, jnp.float32
    return pl.pallas_call(
        functools.partial(chain_kernel, steps, slots, blocks, row_devices),
        out_shape=jax.ShapeDtypeStruct(flat, bf16),
        in_specs=[smem, smem] + [hbm] * 6,
        out_specs=hbm,
        scratch_shapes=[
            pltpu.VMEM(flat, bf16),
            pltpu.VMEM(flat, bf16),
            pltpu.VMEM(flat, bf16),
            pltpu.VMEM((steps, 2 * rows, width), bf16),
            pltpu.VMEM((steps, 2 * rows, width), bf16),
            pltpu.VMEM((steps + 1, 3 * half, width), bf16),
            pltpu.VMEM((steps, 3 * half, width), bf16),
            pltpu.VMEM((2, 3 * half, width), f32),
            pltpu.VMEM((steps, 8, width), f32),
            pltpu.VMEM((steps, 8, width), f32),
            pltpu.VMEM((2 * half, 1), f32),
            pltpu.VMEM((1, width), f32),
            pltpu.VMEM((steps, rows, width), bf16),
            pltpu.VMEM(w_first.shape, bf16),
            pltpu.VMEM(w_third.shape, bf16),
            pltpu.VMEM(w_second.shape, bf16),
            pltpu.SemaphoreType.DMA((8,)),
            pltpu.SemaphoreType.DMA((5, steps)),
            pltpu.SemaphoreType.DMA((5, steps)),
            pltpu.SemaphoreType.DMA((steps,)),
        ],
        compiler_params=pltpu.CompilerParams(
            collective_id=collective_id, has_side_effects=True, vmem_limit_bytes=VMEM_LIMIT
        ),
        cost_estimate=pl.CostEstimate(
            flops=steps * 18 * rows * width * hidden,
            bytes_accessed=4 * 2 * total * rows * width,
            transcendentals=steps * 2 * rows * hidden,
        ),
        name="chain",
    )(
        counts, rate, queries.reshape(flat), keys.reshape(flat), values.reshape(flat),
        w_first, w_third, w_second,
    )


def place_kernel(slots, blocks, counts_ref, in_ref, out_ref, zeros, sems):
    seq = lax.axis_index("seq")
    total = slots * blocks

    def store(source, at):
        return pltpu.make_async_copy(source, out_ref.at[at], sems.at[at])

    live = []
    offset = jnp.int32(0)
    for slot in range(slots):
        count = counts_ref[seq * slots + slot]
        for block in range(blocks):
            at = slot * blocks + block
            live.append(block < count)
            source = jnp.minimum(offset + block, total - 1)
            pl.when(live[at])(lambda: store(in_ref.at[source], at).start())
        offset = offset + count
    zeros[...] = jnp.zeros_like(zeros)
    for at in range(total):
        pl.when(jnp.logical_not(live[at]))(lambda: store(zeros, at).start())
    for at in range(total):
        store(zeros, at).wait()


def place(slots, blocks, counts, in_order):
    return pl.pallas_call(
        functools.partial(place_kernel, slots, blocks),
        out_shape=jax.ShapeDtypeStruct(in_order.shape, in_order.dtype),
        in_specs=[
            pl.BlockSpec(memory_space=pltpu.SMEM), pl.BlockSpec(memory_space=pltpu.VMEM)
        ],
        out_specs=pl.BlockSpec(memory_space=pl.ANY),
        scratch_shapes=[
            pltpu.VMEM(in_order.shape[1:], in_order.dtype),
            pltpu.SemaphoreType.DMA((slots * blocks,)),
        ],
        compiler_params=pltpu.CompilerParams(vmem_limit_bytes=VMEM_LIMIT),
        name="place",
    )(counts, in_order)


def pair_body(queries, keys, values, counts, rate, w_first, w_third, w_second):
    slots, blocks, _, _ = queries.shape
    fewest, most = blocks + slots - 1, slots * blocks
    loads = lax.reduce_window(counts, jnp.int32(0), lax.add, (slots,), (slots,), "VALID")
    longest = jnp.max(loads)
    forms = [functools.partial(chain, steps, steps - fewest) for steps in range(fewest, most + 1)]
    in_order = lax.switch(
        longest - fewest, forms, queries, keys, values, counts, rate, w_first, w_third, w_second
    )
    return place(slots, blocks, counts, in_order).reshape(queries.shape)


def normalize_rows(matrix, epsilon):
    matrix = matrix.astype(jnp.float32)
    return matrix * lax.rsqrt(jnp.mean(matrix * matrix, axis=-1, keepdims=True) + epsilon)


def column_norms(weight):
    return jnp.sqrt(jnp.sum(weight * weight, axis=0) + 1e-06)


def rescale(moved, target):
    return moved * (target[None, :] / column_norms(moved)[None, :])


def product(first_op, second_op):
    return jnp.dot(first_op, second_op, preferred_element_type=jnp.float32)


def contract_rows(first_op, second_op):
    return lax.dot_general(
        first_op, second_op, (((0,), (0,)), ((), ())), preferred_element_type=jnp.float32
    )


def against_rows(first_op, second_op):
    return lax.dot_general(
        first_op, second_op, (((1,), (1,)), ((), ())), preferred_element_type=jnp.float32
    )


def partial_sums(current, key_rows, value_rows):
    key_norm = normalize_rows(key_rows, 1e-06).astype(jnp.bfloat16)
    gate_pre = product(key_norm, current[0])
    up_pre = product(key_norm, current[1])
    gate_sig = jax.nn.sigmoid(gate_pre)
    gate_act = gate_pre * gate_sig
    hidden = (gate_act * up_pre).astype(jnp.bfloat16)
    d_hidden = against_rows(value_rows, current[2])
    d_gate = (d_hidden * up_pre * gate_sig * (1.0 + gate_pre * (1.0 - gate_sig))).astype(
        jnp.bfloat16
    )
    d_up = (d_hidden * gate_act).astype(jnp.bfloat16)
    return (
        contract_rows(key_norm, d_gate),
        contract_rows(key_norm, d_up),
        contract_rows(hidden, value_rows),
    )


def answer(current, query_rows):
    query_norm = normalize_rows(query_rows, 1e-06).astype(jnp.bfloat16)
    out_gate = product(query_norm, current[0])
    out_up = product(query_norm, current[1])
    out_hidden = (out_gate * jax.nn.sigmoid(out_gate) * out_up).astype(jnp.bfloat16)
    return normalize_rows(product(out_hidden, current[2]), 1e-05).astype(jnp.bfloat16)


def body(queries, keys, values, counts, rate, w_first, w_third, w_second):
    seq_slots, blocks, block_rows, head_width = queries.shape
    group_index = lax.axis_index("seq")
    row_devices = lax.axis_size("rows")
    step_rate = rate[0] / (block_rows * row_devices)
    initial = (w_first[0], w_third[0], w_second[0])
    full_master = tuple((weight.astype(jnp.float32) for weight in initial))
    full_targets = tuple((column_norms(weight) for weight in full_master))

    def combine(partials):
        return (
            lax.psum(partials[0].astype(jnp.bfloat16), "rows").astype(jnp.float32),
            lax.psum(partials[1].astype(jnp.bfloat16), "rows").astype(jnp.float32),
            lax.psum(partials[2].astype(jnp.bfloat16), "rows").astype(jnp.float32),
        )

    def refresh(master):
        as_bf16 = tuple((weight.astype(jnp.bfloat16) for weight in master))
        return as_bf16

    def advance(state_pair, step_inputs):
        master, current = state_pair
        query_rows, key_rows, value_rows, restart, is_live = step_inputs
        master = tuple(
            (
                jnp.where(restart, fresh_value, kept_value)
                for fresh_value, kept_value in zip(full_master, master)
            )
        )
        current = tuple(
            (
                jnp.where(restart, fresh_value, kept_value)
                for fresh_value, kept_value in zip(initial, current)
            )
        )
        totals = combine(partial_sums(current, key_rows, value_rows))
        moved = tuple(
            (
                rescale(weight + step_rate * grad_total, target)
                for weight, grad_total, target in zip(master, totals, full_targets)
            )
        )
        master = tuple((jnp.where(is_live, new_w, old_w) for new_w, old_w in zip(moved, master)))
        current = refresh(master)
        output = answer(current, query_rows)
        return ((master, current), jnp.where(is_live, output, jnp.zeros_like(output)))

    start_pair = (full_master, initial)
    flat_shape = (seq_slots * blocks, block_rows, head_width)
    block_ids = jnp.arange(blocks, dtype=jnp.int32)
    local_counts = lax.dynamic_slice_in_dim(counts, group_index * seq_slots, seq_slots)
    restart = jnp.tile(block_ids == 0, seq_slots)
    is_live = (block_ids[None, :] < local_counts[:, None]).reshape(-1)
    inputs = (
        queries.reshape(flat_shape),
        keys.reshape(flat_shape),
        values.reshape(flat_shape),
        restart,
        is_live,
    )
    _, outputs = lax.scan(advance, start_pair, inputs)
    return outputs.reshape(queries.shape)


def any_body(queries, keys, values, counts, rate, w_first, w_third, w_second):
    pair = lax.axis_size("rows") == 2 and w_second.shape[1] % 256 == 0 and queries.shape[2] % 16 == 0
    form = pair_body if pair else body
    return form(queries, keys, values, counts, rate, w_first, w_third, w_second)


def solution(mesh):
    return jax.shard_map(
        any_body,
        mesh=mesh,
        in_specs=(
            P("seq", None, "rows", "head"),
            P("seq", None, "rows", "head"),
            P("seq", None, "rows", "head"),
            P(),
            P("head"),
            P("head", None, None),
            P("head", None, None),
            P("head", None, None),
        ),
        out_specs=P("seq", None, "rows", "head"),
        check_vma=False,
    )
```

```python
import functools

import jax
import jax.numpy as jnp
from jax import lax
from jax.experimental import pallas as pl
from jax.experimental.pallas import tpu as pltpu
from jax.sharding import PartitionSpec as P

MESH = pl.DeviceIdType.MESH
VMEM_LIMIT = 60 * 1024 * 1024


def matmul(first_op, second_op):
    return jnp.dot(first_op, second_op, preferred_element_type=jnp.float32)


def matmul_nt(first_op, second_op):
    return lax.dot_general(
        first_op, second_op, (((1,), (1,)), ((), ())), preferred_element_type=jnp.float32
    )


def unit_rows(matrix, epsilon):
    matrix = matrix.astype(jnp.float32)
    mean = jnp.mean(matrix * matrix, axis=-1, keepdims=True)
    return (matrix * lax.rsqrt(mean + epsilon)).astype(jnp.bfloat16)


def sigmoid(x):
    return 0.5 * jnp.tanh(0.5 * x) + 0.5


def chain_kernel(
    steps, slots, blocks, row_devices,
    counts_ref, rate_ref, q_hbm, k_hbm, v_hbm, w1_hbm, w3_hbm, w2_hbm, out_ref,
    q_in, k_in, v_in, k_all, v_all, n_own, n_peer, state, sums_own, sums_peer,
    norm13, norm2, out_all, w1_ref, w3_ref, w2_ref, load_sem, send_sem, recv_sem, out_sem,
):
    rows = q_in.shape[1]
    half = w2_ref.shape[1] // 2
    me = lax.axis_index("rows")
    peer = {"rows": 1 - me}
    seq = lax.axis_index("seq")
    step_rate = rate_ref[0] / (rows * row_devices)
    total_blocks = slots * blocks

    def local(src, dst, at):
        return pltpu.make_async_copy(src, dst, load_sem.at[at])

    second = sorted({1, blocks} & set(range(total_blocks)))
    edges = [0] + second + [total_blocks]
    ranges = [(low + 1, high - low - 1) for low, high in zip(edges, edges[1:]) if high - low > 1]
    loads, at = [], 0
    for spans in [[(0, 1)], [(block, 1) for block in second], ranges]:
        loads.append([])
        for low, size in spans:
            span = pl.ds(low, size)
            loads[-1].append(local(k_hbm.at[span], k_in.at[span], at))
            loads[-1].append(local(v_hbm.at[span], v_in.at[span], at + 1))
            at += 2
    query_load = local(q_hbm, q_in, at)
    weight_loads = [
        local(w1_hbm, w1_ref, at + 1),
        local(w3_hbm, w3_ref, at + 2),
        local(w2_hbm, w2_ref, at + 3),
    ]
    for load in loads[0] + weight_loads + loads[1]:
        load.start()

    barrier = pltpu.get_barrier_semaphore()
    pl.semaphore_signal(barrier, inc=1, device_id=peer, device_id_type=MESH)

    def where_at(t):
        block = jnp.int32(0)
        begins = t == 0
        offset = jnp.int32(0)
        for slot in range(slots):
            begins = begins | (t == offset)
            inside = jnp.minimum(jnp.maximum(t - offset, 0), blocks - 1)
            block = jnp.where(t >= offset, slot * blocks + inside, block)
            offset = offset + counts_ref[seq * slots + slot]
        return block, begins

    def remote(src, dst, kind, t):
        return pltpu.make_async_remote_copy(
            src_ref=src, dst_ref=dst, send_sem=send_sem.at[kind, t], recv_sem=recv_sem.at[kind, t],
            device_id=peer, device_id_type=MESH,
        )

    mine, theirs = pl.ds(0, rows), pl.ds(rows, rows)
    gates, downs = pl.ds(0, 2 * half), pl.ds(2 * half, half)

    def key_copy(t):
        return remote(k_all.at[t, mine], k_all.at[t, theirs], 0, t)

    def value_copy(t):
        return remote(v_all.at[t, mine], v_all.at[t, theirs], 1, t)

    def sums_copy(t):
        return remote(sums_own.at[t], sums_peer.at[t], 2, t)

    def gates_copy(t):
        return remote(n_own.at[t + 1, gates], n_peer.at[t, gates], 3, t)

    def downs_copy(t):
        return remote(n_own.at[t + 1, downs], n_peer.at[t, downs], 4, t)

    def prepare(t, block):
        v_all[t, mine] = v_in[block]
        k_all[t, mine] = unit_rows(k_in[block], 1e-06)

    def prepare_second():
        taken = where_at(1)[0] == second[0]

        def pick(ref):
            return jnp.where(
                taken, ref[second[0]].astype(jnp.float32), ref[second[-1]].astype(jnp.float32)
            )

        v_all[1, mine] = pick(v_in).astype(jnp.bfloat16)
        k_all[1, mine] = unit_rows(pick(k_in), 1e-06)

    def hand_over(t):
        key_copy(t).start()
        value_copy(t).start()

    def out_copy(t):
        return pltpu.make_async_copy(out_all.at[t], out_ref.at[t], out_sem.at[t])

    pl.semaphore_wait(barrier, 1)
    loads[0][0].wait()
    k_all[0, mine] = unit_rows(k_in[0], 1e-06)
    key_copy(0).start()
    loads[0][1].wait()
    v_all[0, mine] = v_in[0]
    value_copy(0).start()
    for load in loads[2]:
        load.start()
    for load in weight_loads:
        load.wait()

    units = pl.ds(pl.multiple_of(me * half, half), half)
    start_1 = w1_ref[0, :, units].astype(jnp.float32).T
    start_3 = w3_ref[0, :, units].astype(jnp.float32).T
    start_2 = w2_ref[0, units, :].astype(jnp.float32)
    start = jnp.concatenate([start_1, start_3, start_2], axis=0)
    state[0] = start
    n_own[0] = start.astype(jnp.bfloat16)
    start_13 = start[: 2 * half]
    norm13[...] = jnp.sqrt(jnp.sum(start_13 * start_13, axis=1, keepdims=True) + 1e-06)
    full_2 = w2_ref[0].astype(jnp.float32)
    norm2[...] = jnp.sqrt(jnp.sum(full_2 * full_2, axis=0, keepdims=True) + 1e-06)

    def answer(t):
        block, _ = where_at(t)
        query = unit_rows(q_in[block], 1e-06)
        own, other = n_own[t + 1], n_peer[t]
        hidden = []
        for weights in (own, other):
            both = matmul_nt(query, weights[: 2 * half])
            gate, up = both[:, :half], both[:, half:]
            hidden.append((gate * sigmoid(gate) * up).astype(jnp.bfloat16))
        result = matmul(
            jnp.concatenate(hidden, axis=1),
            jnp.concatenate([own[2 * half :], other[2 * half :]], axis=0),
        )
        out_all[t] = unit_rows(result, 1e-05)

    def step(t, has_before, has_after):
        _, begins = where_at(t)
        from_state = jnp.where(begins, 0, 1)
        from_n = jnp.where(begins, 0, t)
        first_step = not has_before and t == 0
        if has_before:
            gates_copy(t - 2).wait_recv()
            downs_copy(t - 2).wait_recv()
        moved_2 = state[from_state, downs]
        moved_13 = state[from_state, gates]
        for part in (mine, theirs) if first_step else (pl.ds(0, 2 * rows),):
            if part is not mine:
                key_copy(t).wait_recv()
                value_copy(t).wait_recv()
            keys, values = k_all[t, part], v_all[t, part]
            both = matmul_nt(n_own[from_n, gates], keys)
            d_hidden = matmul_nt(n_own[from_n, downs], values)
            if first_step and part is theirs:
                for load in loads[2]:
                    load.wait()
                query_load.start()
            if has_after and part is not mine:
                prepare(t + 2, where_at(t + 2)[0])
            gate, up = both[:half], both[half:]
            sig = sigmoid(gate)
            act = gate * sig
            hidden = (act * up).astype(jnp.bfloat16)
            d_gate = (d_hidden * up * (sig + act - act * sig)).astype(jnp.bfloat16)
            d_up = (d_hidden * act).astype(jnp.bfloat16)
            moved_2 = moved_2 + step_rate * matmul(hidden, values)
            if part is mine:
                moved_13 = moved_13 + step_rate * matmul(
                    jnp.concatenate([d_gate, d_up], axis=0), keys
                )
                for load in loads[1]:
                    load.wait()
                if steps > 1:
                    prepare_second()
                    hand_over(1)

        squares = moved_2 * moved_2
        sums_own[t] = jnp.sum(squares.reshape(half // 8, 8, squares.shape[1]), axis=0)
        sums_copy(t).start()
        if has_after:
            hand_over(t + 2)

        moved_13 = moved_13 + step_rate * matmul(jnp.concatenate([d_gate, d_up], axis=0), keys)
        norm = jnp.sum(moved_13 * moved_13, axis=1, keepdims=True) + 1e-06
        new_13 = moved_13 * (norm13[...] * lax.rsqrt(norm))
        state[1, gates] = new_13
        state[1, downs] = moved_2
        n_own[t + 1, gates] = new_13.astype(jnp.bfloat16)
        if has_before:
            answer(t - 2)
        gates_copy(t).start()
        if has_before:
            out_copy(t - 2).start()

        sums_copy(t).wait_recv()
        norm = jnp.sum(sums_own[t] + sums_peer[t], axis=0, keepdims=True) + 1e-06
        new_2 = state[1, downs] * (norm2[...] * lax.rsqrt(norm))
        state[1, downs] = new_2
        n_own[t + 1, downs] = new_2.astype(jnp.bfloat16)
        downs_copy(t).start()

    for t in range(min(2, steps)):
        step(t, False, t + 2 < steps)
    query_load.wait()
    if steps > 4:
        pl.loop(2, steps - 2)(lambda t: step(t, True, True))
    for t in range(max(2, steps - 2), steps):
        step(t, True, False)
    for t in range(max(0, steps - 2), steps):
        gates_copy(t).wait_recv()
        downs_copy(t).wait_recv()
        answer(t)
        out_copy(t).start()

    def finish(t, carry):
        for copy in (key_copy, value_copy, sums_copy, gates_copy, downs_copy):
            copy(t).wait_send()
        out_copy(t).wait()
        return carry

    lax.fori_loop(0, steps, finish, 0)


def chain(steps, collective_id, queries, keys, values, counts, rate, w_first, w_third, w_second):
    slots, blocks, rows, width = queries.shape
    row_devices = lax.axis_size("rows")
    hidden = w_second.shape[1]
    half = hidden // 2
    total = slots * blocks
    flat = (total, rows, width)
    smem = pl.BlockSpec(memory_space=pltpu.SMEM)
    hbm = pl.BlockSpec(memory_space=pl.ANY)
    bf16, f32 = jnp.bfloat16, jnp.float32
    return pl.pallas_call(
        functools.partial(chain_kernel, steps, slots, blocks, row_devices),
        out_shape=jax.ShapeDtypeStruct(flat, bf16),
        in_specs=[smem, smem] + [hbm] * 6,
        out_specs=hbm,
        scratch_shapes=[
            pltpu.VMEM(flat, bf16),
            pltpu.VMEM(flat, bf16),
            pltpu.VMEM(flat, bf16),
            pltpu.VMEM((steps, 2 * rows, width), bf16),
            pltpu.VMEM((steps, 2 * rows, width), bf16),
            pltpu.VMEM((steps + 1, 3 * half, width), bf16),
            pltpu.VMEM((steps, 3 * half, width), bf16),
            pltpu.VMEM((2, 3 * half, width), f32),
            pltpu.VMEM((steps, 8, width), f32),
            pltpu.VMEM((steps, 8, width), f32),
            pltpu.VMEM((2 * half, 1), f32),
            pltpu.VMEM((1, width), f32),
            pltpu.VMEM((steps, rows, width), bf16),
            pltpu.VMEM(w_first.shape, bf16),
            pltpu.VMEM(w_third.shape, bf16),
            pltpu.VMEM(w_second.shape, bf16),
            pltpu.SemaphoreType.DMA((16,)),
            pltpu.SemaphoreType.DMA((5, steps)),
            pltpu.SemaphoreType.DMA((5, steps)),
            pltpu.SemaphoreType.DMA((steps,)),
        ],
        compiler_params=pltpu.CompilerParams(
            collective_id=collective_id, has_side_effects=True, vmem_limit_bytes=VMEM_LIMIT
        ),
        cost_estimate=pl.CostEstimate(
            flops=steps * 18 * rows * width * hidden,
            bytes_accessed=4 * 2 * total * rows * width,
            transcendentals=steps * 2 * rows * hidden,
        ),
        name="chain",
    )(
        counts, rate, queries.reshape(flat), keys.reshape(flat), values.reshape(flat),
        w_first, w_third, w_second,
    )


def place_kernel(slots, blocks, counts_ref, in_ref, out_ref, zeros, sems):
    seq = lax.axis_index("seq")
    total = slots * blocks

    def store(source, at):
        return pltpu.make_async_copy(source, out_ref.at[at], sems.at[at])

    live = []
    offset = jnp.int32(0)
    for slot in range(slots):
        count = counts_ref[seq * slots + slot]
        for block in range(blocks):
            at = slot * blocks + block
            live.append(block < count)
            source = jnp.minimum(offset + block, total - 1)
            pl.when(live[at])(lambda: store(in_ref.at[source], at).start())
        offset = offset + count
    zeros[...] = jnp.zeros_like(zeros)
    for at in range(total):
        pl.when(jnp.logical_not(live[at]))(lambda: store(zeros, at).start())
    for at in range(total):
        store(zeros, at).wait()


def place(slots, blocks, counts, in_order):
    return pl.pallas_call(
        functools.partial(place_kernel, slots, blocks),
        out_shape=jax.ShapeDtypeStruct(in_order.shape, in_order.dtype),
        in_specs=[
            pl.BlockSpec(memory_space=pltpu.SMEM), pl.BlockSpec(memory_space=pltpu.VMEM)
        ],
        out_specs=pl.BlockSpec(memory_space=pl.ANY),
        scratch_shapes=[
            pltpu.VMEM(in_order.shape[1:], in_order.dtype),
            pltpu.SemaphoreType.DMA((slots * blocks,)),
        ],
        compiler_params=pltpu.CompilerParams(vmem_limit_bytes=VMEM_LIMIT),
        name="place",
    )(counts, in_order)


def pair_body(queries, keys, values, counts, rate, w_first, w_third, w_second):
    slots, blocks, _, _ = queries.shape
    fewest, most = blocks + slots - 1, slots * blocks
    loads = lax.reduce_window(counts, jnp.int32(0), lax.add, (slots,), (slots,), "VALID")
    longest = jnp.max(loads)
    forms = [functools.partial(chain, steps, steps - fewest) for steps in range(fewest, most + 1)]
    in_order = lax.switch(
        longest - fewest, forms, queries, keys, values, counts, rate, w_first, w_third, w_second
    )
    return place(slots, blocks, counts, in_order).reshape(queries.shape)


def normalize_rows(matrix, epsilon):
    matrix = matrix.astype(jnp.float32)
    return matrix * lax.rsqrt(jnp.mean(matrix * matrix, axis=-1, keepdims=True) + epsilon)


def column_norms(weight):
    return jnp.sqrt(jnp.sum(weight * weight, axis=0) + 1e-06)


def rescale(moved, target):
    return moved * (target[None, :] / column_norms(moved)[None, :])


def product(first_op, second_op):
    return jnp.dot(first_op, second_op, preferred_element_type=jnp.float32)


def contract_rows(first_op, second_op):
    return lax.dot_general(
        first_op, second_op, (((0,), (0,)), ((), ())), preferred_element_type=jnp.float32
    )


def against_rows(first_op, second_op):
    return lax.dot_general(
        first_op, second_op, (((1,), (1,)), ((), ())), preferred_element_type=jnp.float32
    )


def partial_sums(current, key_rows, value_rows):
    key_norm = normalize_rows(key_rows, 1e-06).astype(jnp.bfloat16)
    gate_pre = product(key_norm, current[0])
    up_pre = product(key_norm, current[1])
    gate_sig = jax.nn.sigmoid(gate_pre)
    gate_act = gate_pre * gate_sig
    hidden = (gate_act * up_pre).astype(jnp.bfloat16)
    d_hidden = against_rows(value_rows, current[2])
    d_gate = (d_hidden * up_pre * gate_sig * (1.0 + gate_pre * (1.0 - gate_sig))).astype(
        jnp.bfloat16
    )
    d_up = (d_hidden * gate_act).astype(jnp.bfloat16)
    return (
        contract_rows(key_norm, d_gate),
        contract_rows(key_norm, d_up),
        contract_rows(hidden, value_rows),
    )


def answer(current, query_rows):
    query_norm = normalize_rows(query_rows, 1e-06).astype(jnp.bfloat16)
    out_gate = product(query_norm, current[0])
    out_up = product(query_norm, current[1])
    out_hidden = (out_gate * jax.nn.sigmoid(out_gate) * out_up).astype(jnp.bfloat16)
    return normalize_rows(product(out_hidden, current[2]), 1e-05).astype(jnp.bfloat16)


def body(queries, keys, values, counts, rate, w_first, w_third, w_second):
    seq_slots, blocks, block_rows, head_width = queries.shape
    group_index = lax.axis_index("seq")
    row_devices = lax.axis_size("rows")
    step_rate = rate[0] / (block_rows * row_devices)
    initial = (w_first[0], w_third[0], w_second[0])
    full_master = tuple((weight.astype(jnp.float32) for weight in initial))
    full_targets = tuple((column_norms(weight) for weight in full_master))

    def combine(partials):
        return (
            lax.psum(partials[0].astype(jnp.bfloat16), "rows").astype(jnp.float32),
            lax.psum(partials[1].astype(jnp.bfloat16), "rows").astype(jnp.float32),
            lax.psum(partials[2].astype(jnp.bfloat16), "rows").astype(jnp.float32),
        )

    def refresh(master):
        as_bf16 = tuple((weight.astype(jnp.bfloat16) for weight in master))
        return as_bf16

    def advance(state_pair, step_inputs):
        master, current = state_pair
        query_rows, key_rows, value_rows, restart, is_live = step_inputs
        master = tuple(
            (
                jnp.where(restart, fresh_value, kept_value)
                for fresh_value, kept_value in zip(full_master, master)
            )
        )
        current = tuple(
            (
                jnp.where(restart, fresh_value, kept_value)
                for fresh_value, kept_value in zip(initial, current)
            )
        )
        totals = combine(partial_sums(current, key_rows, value_rows))
        moved = tuple(
            (
                rescale(weight + step_rate * grad_total, target)
                for weight, grad_total, target in zip(master, totals, full_targets)
            )
        )
        master = tuple((jnp.where(is_live, new_w, old_w) for new_w, old_w in zip(moved, master)))
        current = refresh(master)
        output = answer(current, query_rows)
        return ((master, current), jnp.where(is_live, output, jnp.zeros_like(output)))

    start_pair = (full_master, initial)
    flat_shape = (seq_slots * blocks, block_rows, head_width)
    block_ids = jnp.arange(blocks, dtype=jnp.int32)
    local_counts = lax.dynamic_slice_in_dim(counts, group_index * seq_slots, seq_slots)
    restart = jnp.tile(block_ids == 0, seq_slots)
    is_live = (block_ids[None, :] < local_counts[:, None]).reshape(-1)
    inputs = (
        queries.reshape(flat_shape),
        keys.reshape(flat_shape),
        values.reshape(flat_shape),
        restart,
        is_live,
    )
    _, outputs = lax.scan(advance, start_pair, inputs)
    return outputs.reshape(queries.shape)


def any_body(queries, keys, values, counts, rate, w_first, w_third, w_second):
    pair = lax.axis_size("rows") == 2 and w_second.shape[1] % 256 == 0 and queries.shape[2] % 16 == 0
    form = pair_body if pair else body
    return form(queries, keys, values, counts, rate, w_first, w_third, w_second)


def solution(mesh):
    return jax.shard_map(
        any_body,
        mesh=mesh,
        in_specs=(
            P("seq", None, "rows", "head"),
            P("seq", None, "rows", "head"),
            P("seq", None, "rows", "head"),
            P(),
            P("head"),
            P("head", None, None),
            P("head", None, None),
            P("head", None, None),
        ),
        out_specs=P("seq", None, "rows", "head"),
        check_vma=False,
    )
```

```python
import functools

import jax
import jax.numpy as jnp
from jax import lax
from jax.experimental import pallas as pl
from jax.experimental.pallas import tpu as pltpu
from jax.sharding import PartitionSpec as P

MESH = pl.DeviceIdType.MESH
VMEM_LIMIT = 60 * 1024 * 1024


def matmul(first_op, second_op):
    return jnp.dot(first_op, second_op, preferred_element_type=jnp.float32)


def matmul_nt(first_op, second_op):
    return lax.dot_general(
        first_op, second_op, (((1,), (1,)), ((), ())), preferred_element_type=jnp.float32
    )


def unit_rows(matrix, epsilon):
    matrix = matrix.astype(jnp.float32)
    mean = jnp.mean(matrix * matrix, axis=-1, keepdims=True)
    return (matrix * lax.rsqrt(mean + epsilon)).astype(jnp.bfloat16)


def sigmoid(x):
    return 0.5 * jnp.tanh(0.5 * x) + 0.5


def chain_kernel(
    steps, slots, blocks, row_devices,
    counts_ref, rate_ref, q_hbm, k_hbm, v_hbm, w1_hbm, w3_hbm, w2_hbm, out_ref,
    q_in, k_in, v_in, k_all, v_all, n_own, n_peer, state, sums_own, sums_peer,
    norm13, norm2, out_all, w1_ref, w3_ref, w2_ref, load_sem, send_sem, recv_sem, out_sem,
):
    rows = q_in.shape[1]
    half = w2_ref.shape[1] // 2
    me = lax.axis_index("rows")
    peer = {"rows": 1 - me}
    seq = lax.axis_index("seq")
    step_rate = rate_ref[0] / (rows * row_devices)
    total_blocks = slots * blocks

    def local(src, dst, at):
        return pltpu.make_async_copy(src, dst, load_sem.at[at])

    second = sorted({1, blocks} & set(range(total_blocks)))
    edges = [0] + second + [total_blocks]
    ranges = [(low + 1, high - low - 1) for low, high in zip(edges, edges[1:]) if high - low > 1]
    loads, at = [], 0
    for spans in [[(0, 1)], [(block, 1) for block in second], ranges]:
        loads.append([])
        for low, size in spans:
            span = pl.ds(low, size)
            loads[-1].append(local(k_hbm.at[span], k_in.at[span], at))
            loads[-1].append(local(v_hbm.at[span], v_in.at[span], at + 1))
            at += 2
    query_load = local(q_hbm, q_in, at)
    weight_loads = [
        local(w1_hbm, w1_ref, at + 1),
        local(w3_hbm, w3_ref, at + 2),
        local(w2_hbm, w2_ref, at + 3),
    ]
    for load in loads[0] + weight_loads + loads[1]:
        load.start()

    barrier = pltpu.get_barrier_semaphore()
    pl.semaphore_signal(barrier, inc=1, device_id=peer, device_id_type=MESH)

    def where_at(t):
        block = jnp.int32(0)
        begins = t == 0
        offset = jnp.int32(0)
        for slot in range(slots):
            begins = begins | (t == offset)
            inside = jnp.minimum(jnp.maximum(t - offset, 0), blocks - 1)
            block = jnp.where(t >= offset, slot * blocks + inside, block)
            offset = offset + counts_ref[seq * slots + slot]
        return block, begins

    def remote(src, dst, kind, t):
        return pltpu.make_async_remote_copy(
            src_ref=src, dst_ref=dst, send_sem=send_sem.at[kind, t], recv_sem=recv_sem.at[kind, t],
            device_id=peer, device_id_type=MESH,
        )

    mine, theirs = pl.ds(0, rows), pl.ds(rows, rows)
    gates, downs = pl.ds(0, 2 * half), pl.ds(2 * half, half)

    def key_copy(t):
        return remote(k_all.at[t, mine], k_all.at[t, theirs], 0, t)

    def value_copy(t):
        return remote(v_all.at[t, mine], v_all.at[t, theirs], 1, t)

    def sums_copy(t):
        return remote(sums_own.at[t], sums_peer.at[t], 2, t)

    def gates_copy(t):
        return remote(n_own.at[t + 1, gates], n_peer.at[t, gates], 3, t)

    def downs_copy(t):
        return remote(n_own.at[t + 1, downs], n_peer.at[t, downs], 4, t)

    def prepare(t, block):
        v_all[t, mine] = v_in[block]
        k_all[t, mine] = unit_rows(k_in[block], 1e-06)

    def prepare_second():
        taken = where_at(1)[0] == second[0]

        def pick(ref):
            return jnp.where(
                taken, ref[second[0]].astype(jnp.float32), ref[second[-1]].astype(jnp.float32)
            )

        v_all[1, mine] = pick(v_in).astype(jnp.bfloat16)
        k_all[1, mine] = unit_rows(pick(k_in), 1e-06)

    def hand_over(t):
        key_copy(t).start()
        value_copy(t).start()

    def out_copy(t):
        return pltpu.make_async_copy(out_all.at[t], out_ref.at[t], out_sem.at[t])

    pl.semaphore_wait(barrier, 1)
    loads[0][0].wait()
    k_all[0, mine] = unit_rows(k_in[0], 1e-06)
    key_copy(0).start()
    loads[0][1].wait()
    v_all[0, mine] = v_in[0]
    value_copy(0).start()
    for load in loads[2]:
        load.start()
    for load in weight_loads:
        load.wait()

    units = pl.ds(pl.multiple_of(me * half, half), half)
    start_1 = w1_ref[0, :, units].astype(jnp.float32).T
    start_3 = w3_ref[0, :, units].astype(jnp.float32).T
    start_2 = w2_ref[0, units, :].astype(jnp.float32)
    start = jnp.concatenate([start_1, start_3, start_2], axis=0)
    state[0] = start
    n_own[0] = start.astype(jnp.bfloat16)
    start_13 = start[: 2 * half]
    norm13[...] = jnp.sqrt(jnp.sum(start_13 * start_13, axis=1, keepdims=True) + 1e-06)
    full_2 = w2_ref[0].astype(jnp.float32)
    norm2[...] = jnp.sqrt(jnp.sum(full_2 * full_2, axis=0, keepdims=True) + 1e-06)

    def answer(t):
        block, _ = where_at(t)
        query = unit_rows(q_in[block], 1e-06)
        own, other = n_own[t + 1], n_peer[t]
        hidden = []
        for weights in (own, other):
            both = matmul_nt(query, weights[: 2 * half])
            gate, up = both[:, :half], both[:, half:]
            hidden.append((gate * sigmoid(gate) * up).astype(jnp.bfloat16))
        result = matmul(
            jnp.concatenate(hidden, axis=1),
            jnp.concatenate([own[2 * half :], other[2 * half :]], axis=0),
        )
        out_all[t] = unit_rows(result, 1e-05)

    def step(t, has_before, has_after):
        _, begins = where_at(t)
        from_state = jnp.where(begins, 0, 1)
        from_n = jnp.where(begins, 0, t)
        first_step = not has_before and t == 0
        if has_before:
            gates_copy(t - 2).wait_recv()
            downs_copy(t - 2).wait_recv()
        moved_2 = state[from_state, downs]
        moved_13 = state[from_state, gates]
        for part in (mine, theirs) if first_step else (pl.ds(0, 2 * rows),):
            if part is not mine:
                key_copy(t).wait_recv()
                value_copy(t).wait_recv()
            keys, values = k_all[t, part], v_all[t, part]
            both = matmul_nt(n_own[from_n, gates], keys)
            d_hidden = matmul_nt(n_own[from_n, downs], values)
            if first_step and part is theirs:
                for load in loads[2]:
                    load.wait()
                query_load.start()
            if has_after and part is not mine:
                prepare(t + 2, where_at(t + 2)[0])
            gate, up = both[:half], both[half:]
            sig = sigmoid(gate)
            act = gate * sig
            hidden = (act * up).astype(jnp.bfloat16)
            d_gate = (d_hidden * up * (sig + act - act * sig)).astype(jnp.bfloat16)
            d_up = (d_hidden * act).astype(jnp.bfloat16)
            moved_2 = moved_2 + step_rate * matmul(hidden, values)
            if part is mine:
                moved_13 = moved_13 + step_rate * matmul(
                    jnp.concatenate([d_gate, d_up], axis=0), keys
                )
                for load in loads[1]:
                    load.wait()
                if steps > 1:
                    prepare_second()
                    hand_over(1)

        squares = moved_2 * moved_2
        sums_own[t] = jnp.sum(squares.reshape(half // 8, 8, squares.shape[1]), axis=0)
        sums_copy(t).start()
        if has_after:
            hand_over(t + 2)

        moved_13 = moved_13 + step_rate * matmul(jnp.concatenate([d_gate, d_up], axis=0), keys)
        norm = jnp.sum(moved_13 * moved_13, axis=1, keepdims=True) + 1e-06
        new_13 = moved_13 * (norm13[...] * lax.rsqrt(norm))
        state[1, gates] = new_13
        state[1, downs] = moved_2
        n_own[t + 1, gates] = new_13.astype(jnp.bfloat16)
        if has_before:
            answer(t - 2)
        gates_copy(t).start()
        if has_before:
            out_copy(t - 2).start()

        sums_copy(t).wait_recv()
        norm = jnp.sum(sums_own[t] + sums_peer[t], axis=0, keepdims=True) + 1e-06
        new_2 = state[1, downs] * (norm2[...] * lax.rsqrt(norm))
        state[1, downs] = new_2
        n_own[t + 1, downs] = new_2.astype(jnp.bfloat16)
        downs_copy(t).start()

    for t in range(min(2, steps)):
        step(t, False, t + 2 < steps)
    query_load.wait()
    if steps > 4:
        pl.loop(2, steps - 2)(lambda t: step(t, True, True))
    for t in range(max(2, steps - 2), steps):
        step(t, True, False)
    for t in range(max(0, steps - 2), steps):
        gates_copy(t).wait_recv()
        downs_copy(t).wait_recv()
        answer(t)
        out_copy(t).start()

    def finish(t, carry):
        for copy in (key_copy, value_copy, sums_copy, gates_copy, downs_copy):
            copy(t).wait_send()
        out_copy(t).wait()
        return carry

    lax.fori_loop(0, steps, finish, 0)


def chain(steps, collective_id, queries, keys, values, counts, rate, w_first, w_third, w_second):
    slots, blocks, rows, width = queries.shape
    row_devices = lax.axis_size("rows")
    hidden = w_second.shape[1]
    half = hidden // 2
    total = slots * blocks
    flat = (total, rows, width)
    smem = pl.BlockSpec(memory_space=pltpu.SMEM)
    hbm = pl.BlockSpec(memory_space=pl.ANY)
    bf16, f32 = jnp.bfloat16, jnp.float32
    return pl.pallas_call(
        functools.partial(chain_kernel, steps, slots, blocks, row_devices),
        out_shape=jax.ShapeDtypeStruct(flat, bf16),
        in_specs=[smem, smem] + [hbm] * 6,
        out_specs=hbm,
        scratch_shapes=[
            pltpu.VMEM(flat, bf16),
            pltpu.VMEM(flat, bf16),
            pltpu.VMEM(flat, bf16),
            pltpu.VMEM((steps, 2 * rows, width), bf16),
            pltpu.VMEM((steps, 2 * rows, width), bf16),
            pltpu.VMEM((steps + 1, 3 * half, width), bf16),
            pltpu.VMEM((steps, 3 * half, width), bf16),
            pltpu.VMEM((2, 3 * half, width), f32),
            pltpu.VMEM((steps, 8, width), f32),
            pltpu.VMEM((steps, 8, width), f32),
            pltpu.VMEM((2 * half, 1), f32),
            pltpu.VMEM((1, width), f32),
            pltpu.VMEM((steps, rows, width), bf16),
            pltpu.VMEM(w_first.shape, bf16),
            pltpu.VMEM(w_third.shape, bf16),
            pltpu.VMEM(w_second.shape, bf16),
            pltpu.SemaphoreType.DMA((16,)),
            pltpu.SemaphoreType.DMA((5, steps)),
            pltpu.SemaphoreType.DMA((5, steps)),
            pltpu.SemaphoreType.DMA((steps,)),
        ],
        compiler_params=pltpu.CompilerParams(
            collective_id=collective_id, has_side_effects=True, vmem_limit_bytes=VMEM_LIMIT
        ),
        cost_estimate=pl.CostEstimate(
            flops=steps * 18 * rows * width * hidden,
            bytes_accessed=4 * 2 * total * rows * width,
            transcendentals=steps * 2 * rows * hidden,
        ),
        name="chain",
    )(
        counts, rate, queries.reshape(flat), keys.reshape(flat), values.reshape(flat),
        w_first, w_third, w_second,
    )


def place_kernel(slots, blocks, counts_ref, in_ref, out_ref, zeros, sems):
    seq = lax.axis_index("seq")
    total = slots * blocks

    def store(source, at):
        return pltpu.make_async_copy(source, out_ref.at[at], sems.at[at])

    live = []
    offset = jnp.int32(0)
    for slot in range(slots):
        count = counts_ref[seq * slots + slot]
        for block in range(blocks):
            at = slot * blocks + block
            live.append(block < count)
            source = jnp.minimum(offset + block, total - 1)
            pl.when(live[at])(lambda: store(in_ref.at[source], at).start())
        offset = offset + count
    zeros[...] = jnp.zeros_like(zeros)
    for at in range(total):
        pl.when(jnp.logical_not(live[at]))(lambda: store(zeros, at).start())
    for at in range(total):
        store(zeros, at).wait()


def place(slots, blocks, counts, in_order):
    return pl.pallas_call(
        functools.partial(place_kernel, slots, blocks),
        out_shape=jax.ShapeDtypeStruct(in_order.shape, in_order.dtype),
        in_specs=[
            pl.BlockSpec(memory_space=pltpu.SMEM), pl.BlockSpec(memory_space=pltpu.VMEM)
        ],
        out_specs=pl.BlockSpec(memory_space=pl.ANY),
        scratch_shapes=[
            pltpu.VMEM(in_order.shape[1:], in_order.dtype),
            pltpu.SemaphoreType.DMA((slots * blocks,)),
        ],
        compiler_params=pltpu.CompilerParams(vmem_limit_bytes=VMEM_LIMIT),
        name="place",
    )(counts, in_order)


def pick_kernel(slots, fewest, counts_ref, form_ref):
    longest = jnp.int32(0)
    for start in range(0, counts_ref.shape[0], slots):
        load = jnp.int32(0)
        for slot in range(slots):
            load = load + counts_ref[start + slot]
        longest = jnp.maximum(longest, load)
    form_ref[0] = longest - fewest


def pick_form(slots, fewest, counts):
    smem = pl.BlockSpec(memory_space=pltpu.SMEM)
    return pl.pallas_call(
        functools.partial(pick_kernel, slots, fewest),
        out_shape=jax.ShapeDtypeStruct((1,), jnp.int32),
        in_specs=[smem],
        out_specs=smem,
        name="pick_form",
    )(counts)


def pair_body(queries, keys, values, counts, rate, w_first, w_third, w_second):
    slots, blocks, _, _ = queries.shape
    fewest, most = blocks + slots - 1, slots * blocks
    forms = [functools.partial(chain, steps, steps - fewest) for steps in range(fewest, most + 1)]
    in_order = lax.switch(
        pick_form(slots, fewest, counts)[0], forms, queries, keys, values, counts, rate, w_first, w_third, w_second
    )
    return place(slots, blocks, counts, in_order).reshape(queries.shape)


def normalize_rows(matrix, epsilon):
    matrix = matrix.astype(jnp.float32)
    return matrix * lax.rsqrt(jnp.mean(matrix * matrix, axis=-1, keepdims=True) + epsilon)


def column_norms(weight):
    return jnp.sqrt(jnp.sum(weight * weight, axis=0) + 1e-06)


def rescale(moved, target):
    return moved * (target[None, :] / column_norms(moved)[None, :])


def product(first_op, second_op):
    return jnp.dot(first_op, second_op, preferred_element_type=jnp.float32)


def contract_rows(first_op, second_op):
    return lax.dot_general(
        first_op, second_op, (((0,), (0,)), ((), ())), preferred_element_type=jnp.float32
    )


def against_rows(first_op, second_op):
    return lax.dot_general(
        first_op, second_op, (((1,), (1,)), ((), ())), preferred_element_type=jnp.float32
    )


def partial_sums(current, key_rows, value_rows):
    key_norm = normalize_rows(key_rows, 1e-06).astype(jnp.bfloat16)
    gate_pre = product(key_norm, current[0])
    up_pre = product(key_norm, current[1])
    gate_sig = jax.nn.sigmoid(gate_pre)
    gate_act = gate_pre * gate_sig
    hidden = (gate_act * up_pre).astype(jnp.bfloat16)
    d_hidden = against_rows(value_rows, current[2])
    d_gate = (d_hidden * up_pre * gate_sig * (1.0 + gate_pre * (1.0 - gate_sig))).astype(
        jnp.bfloat16
    )
    d_up = (d_hidden * gate_act).astype(jnp.bfloat16)
    return (
        contract_rows(key_norm, d_gate),
        contract_rows(key_norm, d_up),
        contract_rows(hidden, value_rows),
    )


def answer(current, query_rows):
    query_norm = normalize_rows(query_rows, 1e-06).astype(jnp.bfloat16)
    out_gate = product(query_norm, current[0])
    out_up = product(query_norm, current[1])
    out_hidden = (out_gate * jax.nn.sigmoid(out_gate) * out_up).astype(jnp.bfloat16)
    return normalize_rows(product(out_hidden, current[2]), 1e-05).astype(jnp.bfloat16)


def body(queries, keys, values, counts, rate, w_first, w_third, w_second):
    seq_slots, blocks, block_rows, head_width = queries.shape
    group_index = lax.axis_index("seq")
    row_devices = lax.axis_size("rows")
    step_rate = rate[0] / (block_rows * row_devices)
    initial = (w_first[0], w_third[0], w_second[0])
    full_master = tuple((weight.astype(jnp.float32) for weight in initial))
    full_targets = tuple((column_norms(weight) for weight in full_master))

    def combine(partials):
        return (
            lax.psum(partials[0].astype(jnp.bfloat16), "rows").astype(jnp.float32),
            lax.psum(partials[1].astype(jnp.bfloat16), "rows").astype(jnp.float32),
            lax.psum(partials[2].astype(jnp.bfloat16), "rows").astype(jnp.float32),
        )

    def refresh(master):
        as_bf16 = tuple((weight.astype(jnp.bfloat16) for weight in master))
        return as_bf16

    def advance(state_pair, step_inputs):
        master, current = state_pair
        query_rows, key_rows, value_rows, restart, is_live = step_inputs
        master = tuple(
            (
                jnp.where(restart, fresh_value, kept_value)
                for fresh_value, kept_value in zip(full_master, master)
            )
        )
        current = tuple(
            (
                jnp.where(restart, fresh_value, kept_value)
                for fresh_value, kept_value in zip(initial, current)
            )
        )
        totals = combine(partial_sums(current, key_rows, value_rows))
        moved = tuple(
            (
                rescale(weight + step_rate * grad_total, target)
                for weight, grad_total, target in zip(master, totals, full_targets)
            )
        )
        master = tuple((jnp.where(is_live, new_w, old_w) for new_w, old_w in zip(moved, master)))
        current = refresh(master)
        output = answer(current, query_rows)
        return ((master, current), jnp.where(is_live, output, jnp.zeros_like(output)))

    start_pair = (full_master, initial)
    flat_shape = (seq_slots * blocks, block_rows, head_width)
    block_ids = jnp.arange(blocks, dtype=jnp.int32)
    local_counts = lax.dynamic_slice_in_dim(counts, group_index * seq_slots, seq_slots)
    restart = jnp.tile(block_ids == 0, seq_slots)
    is_live = (block_ids[None, :] < local_counts[:, None]).reshape(-1)
    inputs = (
        queries.reshape(flat_shape),
        keys.reshape(flat_shape),
        values.reshape(flat_shape),
        restart,
        is_live,
    )
    _, outputs = lax.scan(advance, start_pair, inputs)
    return outputs.reshape(queries.shape)


def any_body(queries, keys, values, counts, rate, w_first, w_third, w_second):
    pair = lax.axis_size("rows") == 2 and w_second.shape[1] % 256 == 0 and queries.shape[2] % 16 == 0
    form = pair_body if pair else body
    return form(queries, keys, values, counts, rate, w_first, w_third, w_second)


def solution(mesh):
    return jax.shard_map(
        any_body,
        mesh=mesh,
        in_specs=(
            P("seq", None, "rows", "head"),
            P("seq", None, "rows", "head"),
            P("seq", None, "rows", "head"),
            P(),
            P("head"),
            P("head", None, None),
            P("head", None, None),
            P("head", None, None),
        ),
        out_specs=P("seq", None, "rows", "head"),
        check_vma=False,
    )
```
